32 devices in a mesh: row: 8 (over z, x), col: 4 (over y, core).
Axes of the slice: x: 2, y: 2, z: 4, core: 2. Of those that a mesh axis runs over, the one named last changes fastest.
Arguments:
- positions: float32 [3, 65536], P(None, ('row', 'col')), may hold values from -6 to 6
- velocities: float32 [3, 65536], P(None, ('row', 'col')), may hold values from -4 to 4
- pair_lists: int32 [8, 4, 256, 2], P('row', 'col'), may hold values from 0 to 127, as said below
- pair_counts: int32 [8, 4], P('row', 'col'), may hold values from 64 to 256, as said below
Outputs:
- positions_out: float32 [3, 65536], P(None, ('row', 'col'))
- velocities_out: float32 [3, 65536], P(None, ('row', 'col'))
The draws below stay inside these ranges and needn't reach their ends.
Inputs may be any that keep to these rules, and one draw needn't show every extreme that they name: `pair_lists`: entry [r, c, s] holds a row block in its first place and a column block in its second; slots at or past pair_counts[r, c] hold zeros. Blocks may repeat. `pair_counts`: the first entries of pair_lists are below 64. Some device lists exactly 256 pairs.
All inputs are finite; a program needn't handle non-finite values.
Results may differ from the reference program's by a relative error of at most 0.0003.
Values sent between devices are 32-bit elements; how exact they have to be, the bound alone decides.
No kernel may reach another device: no remote copies, remote signals or barrier semaphores. Data moves between devices by JAX's collectives and lax.ppermute only.
A program may use at most 128 MiB of HBM per device.

```python
import jax
import jax.numpy as jnp
from jax import lax

ATOM_DEV = 2048
PAIRS_MAX = 256
STEPS = 3
NATOMS = 65536
BR = 64
BC = 128
N_ROW = 8
N_COL = 4


def draw_shared(key):
    base = jax.random.fold_in(key, 7)
    count_key = jax.random.fold_in(base, 1)
    pick_key = jax.random.fold_in(base, 2)
    left_key = jax.random.fold_in(base, 3)
    right_key = jax.random.fold_in(base, 4)
    counts = jax.random.randint(count_key, (N_ROW * N_COL,), PAIRS_MAX // 4, PAIRS_MAX + 1, dtype=jnp.int32)
    chosen = jax.random.randint(pick_key, (), 0, N_ROW * N_COL, dtype=jnp.int32)
    counts = jnp.where(jnp.arange(N_ROW * N_COL, dtype=jnp.int32) == chosen, PAIRS_MAX, counts)
    counts = counts.reshape(N_ROW, N_COL)
    left_ids = jax.random.randint(left_key, (N_ROW, N_COL, PAIRS_MAX), 0, BR, dtype=jnp.int32)
    right_ids = jax.random.randint(right_key, (N_ROW, N_COL, PAIRS_MAX), 0, BC, dtype=jnp.int32)
    slots = jnp.arange(PAIRS_MAX, dtype=jnp.int32)[None, None, :]
    live = slots < counts[:, :, None]
    left_ids = jnp.where(live, left_ids, 0)
    right_ids = jnp.where(live, right_ids, 0)
    return (jnp.stack([left_ids, right_ids], axis=3), counts)


def draw_pair_lists(key, part):
    lists, counts = draw_shared(key)
    return lists


def draw_pair_counts(key, part):
    lists, counts = draw_shared(key)
    return counts


def block_levels(stream_key, dims, cuts, least, high):
    def one(position, blocks):
        draws = jax.random.uniform(jax.random.fold_in(jax.random.fold_in(stream_key, 6), position), (blocks,), jnp.float32, least / len(cuts), high / len(cuts))
        return jnp.repeat(jnp.exp(draws), dims[position] // blocks).reshape((-1,) + (1,) * (len(dims) - position - 1))

    gain = one(*cuts[0])
    for cut in cuts[1:]:
        gain = gain * one(*cut)
    return gain


def centred(own_key, dims, width, most, shards=(), held_as=jnp.bfloat16):
    values = width * jax.random.normal(own_key, dims, jnp.float32)
    if shards:
        values = values * block_levels(own_key, dims, shards, -0.22, 0.18)
    return jnp.clip(values, -most, most).astype(held_as)


def setup_inputs(seed: int = 0) -> dict:
    splits = jax.random.split(jax.random.key(seed), 5)
    positions = centred(splits[0], (3, NATOMS), 1.0, 6.0, ((1, 32),), jnp.float32)
    velocities = centred(splits[1], (3, NATOMS), 0.5, 4.0, ((1, 32),), jnp.float32)
    pair_lists = draw_pair_lists(jax.random.fold_in(splits[4], 71), 0)
    pair_counts = draw_pair_counts(jax.random.fold_in(splits[4], 71), 0)
    return {"positions": positions, "velocities": velocities, "pair_lists": pair_lists, "pair_counts": pair_counts}


CUTOFF_SQ = 4.0
TIME_STEP = 0.5


def pair_terms(left_tiles, right_tiles, stiffness):
    separation = left_tiles[:, :, :, None] - right_tiles[:, :, None, :]
    distance_sq = jnp.sum(separation * separation, 0)
    weight = stiffness * jnp.maximum(0.0, 1.0 - distance_sq / CUTOFF_SQ)
    weighted = weight[None] * separation
    return jnp.sum(weighted, 3), -jnp.sum(weighted, 2)


def reference(positions, velocities, pair_lists, pair_counts):
    stiffness = ATOM_DEV / (2048.0 * PAIRS_MAX)
    row_ids = jnp.arange(N_ROW, dtype=jnp.int32)[:, None, None] + jnp.zeros((N_ROW, N_COL, PAIRS_MAX), jnp.int32)
    col_ids = jnp.arange(N_COL, dtype=jnp.int32)[None, :, None] + jnp.zeros((N_ROW, N_COL, PAIRS_MAX), jnp.int32)
    slot_ids = jnp.arange(PAIRS_MAX, dtype=jnp.int32)[None, None, :] + jnp.zeros((N_ROW, N_COL, PAIRS_MAX), jnp.int32)
    live = (slot_ids < pair_counts[:, :, None]).reshape(N_ROW * N_COL, PAIRS_MAX)
    left_start = (row_ids * N_COL * ATOM_DEV + pair_lists[..., 0] * 128).reshape(N_ROW * N_COL, PAIRS_MAX).astype(jnp.int32)
    col_offset = pair_lists[..., 1] * 128
    right_start = (((col_offset // ATOM_DEV) * N_COL + col_ids) * ATOM_DEV + col_offset % ATOM_DEV).reshape(N_ROW * N_COL, PAIRS_MAX).astype(jnp.int32)
    lane = jnp.arange(128, dtype=jnp.int32)

    def forces(current):
        def add_group(total, item):
            starts_left, starts_right, valid = item
            left_index = (starts_left[:, None] + lane[None, :]).astype(jnp.int32)
            right_index = (starts_right[:, None] + lane[None, :]).astype(jnp.int32)
            left_tiles = current[:, left_index]
            right_tiles = current[:, right_index]
            left_term, right_term = pair_terms(left_tiles, right_tiles, stiffness)
            scale = valid.astype(total.dtype)
            distinct = (starts_left != starts_right).astype(total.dtype)
            left_term = left_term * scale[None, :, None]
            right_term = right_term * (scale * distinct)[None, :, None]
            total = total.at[:, left_index.reshape(-1)].add(left_term.reshape(3, -1))
            total = total.at[:, right_index.reshape(-1)].add(right_term.reshape(3, -1))
            return total, None

        total, _ = lax.scan(add_group, jnp.zeros_like(current), (left_start, right_start, live))
        return total

    current = positions
    velocity = velocities
    force_now = forces(current)
    for turn in range(STEPS):
        current = current + TIME_STEP * velocity + 0.5 * TIME_STEP * TIME_STEP * force_now
        force_next = forces(current)
        velocity = velocity + 0.5 * TIME_STEP * (force_now + force_next)
        force_now = force_next
    return current, velocity
```

```python
import functools

import jax
import jax.numpy as jnp
from jax import lax
from jax.experimental import pallas as pl
from jax.experimental.pallas import tpu as pltpu
from jax.sharding import PartitionSpec as P

ATOM_DEV = 2048
PAIRS_MAX = 256
STEPS = 3
TIME_STEP = 0.5
STIFFNESS = ATOM_DEV / (2048.0 * PAIRS_MAX)

LANES = 128
LIST_ROWS = 8
UNROLL = 4
FAR = 1.0e6
AXES = ("row", "col")


def stage_masks(devices):
    bits = devices.bit_length() - 1
    groups = [(0, 1)] if bits else []
    low = 1
    while low < bits:
        high = min(low + 2, bits)
        groups.append((low, high))
        low = high
    return [(lo, 1 << (hi - lo)) for lo, hi in reversed(groups)]


def gather(block, devices):
    for low, count in stage_masks(devices):
        parts = [block]
        for step in range(1, count):
            pairs = [(d, d ^ (step << low)) for d in range(devices)]
            parts.append(lax.ppermute(block, AXES, pairs))
        block = jnp.concatenate(parts, 0)
    return block


def slot_of(relative, devices):
    slot = jnp.zeros_like(relative)
    stride = 1
    for low, count in stage_masks(devices):
        slot = slot + ((relative >> low) & (count - 1)) * stride
        stride *= count
    return slot


def sort_list(keys, values, highest):
    slots = keys.shape[0]
    order = jnp.arange(slots, dtype=jnp.int32)
    tagged = keys * slots + order
    rank = jnp.sum((tagged[None, :] < tagged[:, None]).astype(jnp.int32), 1)
    placed = jnp.sum(jnp.where(rank[:, None] == order[None, :], values[:, None], 0), 0)
    ends = jnp.sum((keys[:, None] <= jnp.arange(highest, dtype=jnp.int32)[None, :]).astype(jnp.int32), 0)
    return placed, ends


def list_rows(vector):
    rows = -(-vector.shape[0] // LANES)
    return jnp.pad(vector, (0, rows * LANES - vector.shape[0])).reshape(rows, LANES)


def pack_lists(pairs, total, row, col, nrow, ncol, blocks):
    left, right = pairs[:, 0], pairs[:, 1]
    valid = jnp.arange(pairs.shape[0], dtype=jnp.int32) < total
    left_block = row * ncol * blocks + left
    right_block = ((right // blocks) * ncol + col) * blocks + right % blocks
    none = jnp.int32(1 << 16)
    by_left, left_ends = sort_list(jnp.where(valid, left, none), right_block, ncol * blocks)
    by_right, right_ends = sort_list(
        jnp.where(valid & (left_block != right_block), right, none), left_block, nrow * blocks
    )
    rows = jnp.concatenate([list_rows(v) for v in (by_left, by_right, left_ends, right_ends)], 0)
    return rows.astype(jnp.float32)


def split3(tile):
    high = tile.astype(jnp.bfloat16).astype(jnp.float32)
    rest = tile - high
    mid = rest.astype(jnp.bfloat16).astype(jnp.float32)
    return high, mid, rest - mid


def evaluate(size, gathered, rows, points, lefts, sums, lst, owner, count):
    devices, blocks = size
    stride = 4 * blocks
    for slot in range(devices):
        norm = None
        for c in range(3):
            y = 0.5 * gathered[pl.ds(slot * rows + c * blocks, blocks), :]
            points[pl.ds(slot * stride + c * blocks, blocks), :] = y
            norm = y * y if norm is None else norm + y * y
        points[pl.ds(slot * stride + 3 * blocks, blocks), :] = norm
    points[pl.ds(devices * stride, 3 * blocks), :] = jnp.zeros((3 * blocks, LANES), jnp.float32)
    points[pl.ds(devices * stride + 3 * blocks, blocks), :] = jnp.full((blocks, LANES), FAR, jnp.float32)

    place = lax.broadcasted_iota(jnp.int32, (8, LANES), 0)
    for b in range(blocks):
        tile = points[pl.ds(b, 8, stride=blocks), :]
        moved = pltpu.roll(tile, 1, 0)
        tile = jnp.where(
            place < 3, 2.0 * tile, jnp.where(place == 3, -1.0, jnp.where(place == 4, 1.0 - moved, 0.0))
        )
        high, mid, low = split3(tile)
        stack = jnp.concatenate([high, high, high, mid, mid, low], 0)
        lefts[b] = stack.T.astype(jnp.bfloat16)
    sums[...] = jnp.zeros_like(sums)

    def right_tile(base):
        tile = points[pl.ds(base, 8, stride=blocks), :]
        tile = jnp.where(place < 4, tile, jnp.where(place == 4, 1.0, 0.0))
        high, mid, low = split3(tile)
        return jnp.concatenate([high, mid, low, high, mid, high], 0).astype(jnp.bfloat16)

    def group(number, carry):
        for k in range(UNROLL):
            unit = number * UNROLL + k
            mine = owner[unit]
            right = jnp.concatenate([right_tile(lst[2 * unit]), right_tile(lst[2 * unit + 1])], 1)
            u = lax.dot_general(lefts[mine], right, (((1,), (0,)), ((), ())), preferred_element_type=jnp.float32)
            w = jnp.maximum(u, 0.0)
            w_high = w.astype(jnp.bfloat16)
            w_low = (w - w_high.astype(jnp.float32)).astype(jnp.bfloat16)
            dims = (((1,), (1,)), ((), ()))
            part = lax.dot_general(right[:32], w_high, dims, preferred_element_type=jnp.float32)
            part = part + lax.dot_general(right[:32], w_low, dims, preferred_element_type=jnp.float32)
            at = pl.ds(pl.multiple_of(mine * 32, 32), 32)
            sums[at, :] = sums[at, :] + part
        return carry

    lax.fori_loop(0, (count[0] + UNROLL - 1) // UNROLL, group, 0)

    total = sums[pl.ds(4, blocks, stride=32), :]
    forces = []
    for c in range(3):
        y = points[pl.ds(c * blocks, blocks), :]
        mix = (
            sums[pl.ds(c, blocks, stride=32), :]
            + sums[pl.ds(8 + c, blocks, stride=32), :]
            + sums[pl.ds(16 + c, blocks, stride=32), :]
        )
        forces.append((2.0 * STIFFNESS) * (y * total - mix))
    return forces


def build_units(sources, spans, blocks, dummy, lst, owner, count):
    def one_block(o, carry):
        filled, starts = carry
        first = filled
        ends = []
        for n, (list_row, end_row) in enumerate(spans):
            key = sources[1][n] + o
            end = sources[0][end_row + key // LANES, key % LANES]

            def put(s, at, list_row=list_row):
                lst[at] = sources[0][list_row + s // LANES, s % LANES]
                return at + 1

            filled = lax.fori_loop(starts[n], end, put, filled)
            ends.append(end)
        lst[filled] = dummy
        filled = filled + (filled & 1)

        def own(u, c):
            owner[u] = o
            return c

        lax.fori_loop(first // 2, filled // 2, own, 0)
        return filled, tuple(ends)

    starts = []
    for n, (list_row, end_row) in enumerate(spans):
        key = jnp.maximum(sources[1][n] - 1, 0)
        before = sources[0][end_row + key // LANES, key % LANES]
        starts.append(jnp.where(sources[1][n] > 0, before, 0))
    filled, _ = lax.fori_loop(0, blocks, one_block, (jnp.int32(0), tuple(starts)))
    units = filled // 2
    count[0] = units
    for k in range(UNROLL - 1):
        owner[units + k] = 0
        lst[2 * (units + k)] = dummy
        lst[2 * (units + k) + 1] = dummy


def first_kernel(size, shape, gathered, velocity, x_next, force_out, lst, owner, count, points, lefts, sums, ints, scal, sem):
    devices, blocks = size
    nrow, ncol, slots = shape
    rows = 3 * blocks + LIST_ROWS
    row, col = lax.axis_index("row"), lax.axis_index("col")
    me = row * ncol + col
    list_span = slots // LANES
    holders = [row * ncol + c for c in range(ncol)] + [r * ncol + col for r in range(nrow)]
    for n, holder in enumerate(holders):
        slot = slot_of(holder ^ me, devices)
        tile = gathered[pl.ds(pl.multiple_of(slot * rows + 3 * blocks, 8), LIST_ROWS), :].astype(jnp.int32)
        who = slot_of((tile // blocks) ^ me, devices)
        base = who * (4 * blocks) + tile % blocks
        place = lax.broadcasted_iota(jnp.int32, (LIST_ROWS, LANES), 0)
        ints[pl.ds(n * LIST_ROWS, LIST_ROWS), :] = jnp.where(place < 2 * list_span, base, tile)
    copy = pltpu.make_async_copy(ints, scal, sem)
    copy.start()
    copy.wait()
    left_end = 2 * list_span
    right_end = left_end + -(-ncol * blocks // LANES)
    spans, keys = [], []
    for n in range(ncol):
        spans.append((n * LIST_ROWS, n * LIST_ROWS + left_end))
        keys.append(col * blocks)
    for n in range(ncol, ncol + nrow):
        spans.append((n * LIST_ROWS + list_span, n * LIST_ROWS + right_end))
        keys.append(row * blocks)
    build_units((scal, keys), spans, blocks, devices * 4 * blocks, lst, owner, count)
    forces = evaluate(size, gathered, rows, points, lefts, sums, lst, owner, count)
    for c in range(3):
        at = pl.ds(c * blocks, blocks)
        force_out[at, :] = forces[c]
        x_next[at, :] = gathered[at, :] + TIME_STEP * velocity[at, :] + (0.5 * TIME_STEP * TIME_STEP) * forces[c]


def next_kernel(size, last, gathered, velocity, force, lst, owner, count, x_next, v_next, *rest):
    devices, blocks = size
    if last:
        points, lefts, sums = rest
    else:
        force_out, points, lefts, sums = rest
    forces = evaluate(size, gathered, 3 * blocks, points, lefts, sums, lst, owner, count)
    for c in range(3):
        at = pl.ds(c * blocks, blocks)
        x = gathered[at, :]
        v = velocity[at, :] + (0.5 * TIME_STEP) * (force[at, :] + forces[c])
        v_next[at, :] = v
        if last:
            x_next[at, :] = x
        else:
            force_out[at, :] = forces[c]
            x_next[at, :] = x + TIME_STEP * v + (0.5 * TIME_STEP * TIME_STEP) * forces[c]


def body(positions, velocities, pair_lists, pair_counts):
    nrow, ncol = lax.axis_size("row"), lax.axis_size("col")
    row, col = lax.axis_index("row"), lax.axis_index("col")
    devices = nrow * ncol
    blocks = positions.shape[1] // LANES
    pairs = pair_lists[0, 0]
    slots = pairs.shape[0]
    size = (devices, blocks)
    capacity = (nrow + ncol) * slots // 2 + blocks + UNROLL

    lists = pack_lists(pairs, pair_counts[0, 0], row, col, nrow, ncol, blocks)
    lists = jnp.pad(lists, ((0, LIST_ROWS - lists.shape[0]), (0, 0)))
    current = positions.reshape(3 * blocks, LANES)
    velocity = velocities.reshape(3 * blocks, LANES)

    flat = jax.ShapeDtypeStruct((3 * blocks, LANES), jnp.float32)
    units = [
        jax.ShapeDtypeStruct((2 * capacity,), jnp.int32),
        jax.ShapeDtypeStruct((capacity,), jnp.int32),
        jax.ShapeDtypeStruct((1,), jnp.int32),
    ]
    vmem = pl.BlockSpec(memory_space=pltpu.VMEM)
    smem = pl.BlockSpec(memory_space=pltpu.SMEM)
    scratch = [
        pltpu.VMEM(((devices + 3) * 4 * blocks, LANES), jnp.float32),
        pltpu.VMEM((blocks, LANES, 48), jnp.bfloat16),
        pltpu.VMEM((blocks * 32, LANES), jnp.float32),
    ]
    params = pltpu.CompilerParams(vmem_limit_bytes=48 * 1024 * 1024)

    gathered = gather(jnp.concatenate([current, lists], 0), devices)
    current, force, lst, owner, count = pl.pallas_call(
        functools.partial(first_kernel, size, (nrow, ncol, slots)),
        out_shape=[flat, flat] + units,
        in_specs=[vmem, vmem],
        out_specs=[vmem, vmem, smem, smem, smem],
        scratch_shapes=scratch
        + [
            pltpu.VMEM(((nrow + ncol) * LIST_ROWS, LANES), jnp.int32),
            pltpu.SMEM(((nrow + ncol) * LIST_ROWS, LANES), jnp.int32),
            pltpu.SemaphoreType.DMA,
        ],
        compiler_params=params,
        name="first_forces",
    )(gathered, velocity)
    for turn in range(STEPS):
        last = turn == STEPS - 1
        result = pl.pallas_call(
            functools.partial(next_kernel, size, last),
            out_shape=[flat] * (2 if last else 3),
            in_specs=[vmem, vmem, vmem, smem, smem, smem],
            out_specs=[vmem] * (2 if last else 3),
            scratch_shapes=scratch,
            compiler_params=params,
            name="last_forces" if last else "next_forces",
        )(gather(current, devices), velocity, force, lst, owner, count)
        if last:
            current, velocity = result
        else:
            current, velocity, force = result
    return current.reshape(positions.shape), velocity.reshape(velocities.shape)


def solution(mesh):
    placed = (
        P(None, ("row", "col")),
        P(None, ("row", "col")),
        P("row", "col", None, None),
        P("row", "col"),
    )
    return jax.shard_map(
        body,
        mesh=mesh,
        in_specs=placed,
        out_specs=(P(None, ("row", "col")), P(None, ("row", "col"))),
        check_vma=False,
    )
```

```python
import functools

import jax
import jax.numpy as jnp
from jax import lax
from jax.experimental import pallas as pl
from jax.experimental.pallas import tpu as pltpu
from jax.sharding import PartitionSpec as P

ATOM_DEV = 2048
PAIRS_MAX = 256
STEPS = 3
TIME_STEP = 0.5
STIFFNESS = ATOM_DEV / (2048.0 * PAIRS_MAX)

LANES = 128
LIST_ROWS = 8
UNROLL = 16
BASE_MASK = (1 << 14) - 1
FAR = 1.0e6
AXES = ("row", "col")


def stage_masks(devices):
    bits = devices.bit_length() - 1
    groups = [(0, 1)] if bits else []
    low = 1
    while low < bits:
        high = min(low + 2, bits)
        groups.append((low, high))
        low = high
    return [(lo, 1 << (hi - lo)) for lo, hi in reversed(groups)]


def gather(block, devices):
    for low, count in stage_masks(devices):
        parts = [block]
        for step in range(1, count):
            pairs = [(d, d ^ (step << low)) for d in range(devices)]
            parts.append(lax.ppermute(block, AXES, pairs))
        block = jnp.concatenate(parts, 0)
    return block


def slot_of(relative, devices):
    slot = jnp.zeros_like(relative)
    stride = 1
    for low, count in stage_masks(devices):
        slot = slot + ((relative >> low) & (count - 1)) * stride
        stride *= count
    return slot


def pack_list(pairs, total, span):
    valid = jnp.arange(pairs.shape[0], dtype=jnp.int32) < total
    code = jnp.where(valid, pairs[:, 0] * span + pairs[:, 1], -1).astype(jnp.float32)
    rows = code.reshape(-1, LANES)
    return jnp.pad(rows, ((0, LIST_ROWS - rows.shape[0]), (0, 0)))


def matmul(a, b):
    return jnp.dot(a, b, preferred_element_type=jnp.float32)


def split3(tile):
    high = tile.astype(jnp.bfloat16).astype(jnp.float32)
    rest = tile - high
    mid = rest.astype(jnp.bfloat16).astype(jnp.float32)
    return high, mid, rest - mid


def evaluate(size, gathered, rows, units, points, lefts, sums):
    devices, blocks = size
    stride = 4 * blocks
    dummy = devices * stride
    for slot in range(devices):
        norm = None
        for c in range(3):
            y = 0.5 * gathered[pl.ds(slot * rows + c * blocks, blocks), :]
            points[pl.ds(slot * stride + c * blocks, blocks), :] = y
            norm = y * y if norm is None else norm + y * y
        points[pl.ds(slot * stride + 3 * blocks, blocks), :] = norm
    points[pl.ds(dummy, 3 * blocks), :] = jnp.zeros((3 * blocks, LANES), jnp.float32)
    points[pl.ds(dummy + 3 * blocks, blocks), :] = jnp.full((blocks, LANES), FAR, jnp.float32)

    place = lax.broadcasted_iota(jnp.int32, (8, LANES), 0)
    for b in range(blocks):
        tile = points[pl.ds(b, 8, stride=blocks), :]
        moved = pltpu.roll(tile, 1, 0)
        tile = jnp.where(
            place < 3, 2.0 * tile, jnp.where(place == 3, -1.0, jnp.where(place == 4, 1.0 - moved, 0.0))
        )
        high, mid, low = split3(tile)
        lefts[b] = jnp.concatenate([high, high, high, mid, mid, low], 0).astype(jnp.bfloat16)
    sums[...] = jnp.zeros_like(sums)

    def right_tile(word):
        tile = points[pl.ds(dummy - (word & BASE_MASK), 8, stride=blocks), :]
        tile = jnp.where(place < 4, tile, jnp.where(place == 4, 1.0, 0.0))
        high, mid, low = split3(tile)
        return jnp.concatenate([high, mid, low, high, mid, high], 0).astype(jnp.bfloat16)

    def group(number, carry):
        staged = []
        for k in range(UNROLL):
            at = 2 * (number * UNROLL + k)
            words = [units[(at + n) // LANES, (at + n) % LANES] for n in range(2)]
            rights = [right_tile(word) for word in words]
            mine = words[0] // (BASE_MASK + 1)
            u = matmul(jnp.concatenate([r.T for r in rights], 0), lefts[mine])
            staged.append((mine, jnp.concatenate([r[:32] for r in rights], 1), u))
        parts = []
        for mine, right, u in staged:
            w = jnp.maximum(u, 0.0)
            high = w.astype(jnp.bfloat16)
            low = (w - high.astype(jnp.float32)).astype(jnp.bfloat16)
            part = matmul(right, jnp.concatenate([high, low], 1))
            parts.append(part[:, :LANES] + part[:, LANES:])
        for (mine, _, _), part in zip(staged, parts):
            at = pl.ds(pl.multiple_of(mine * 32, 32), 32)
            sums[at, :] = sums[at, :] + part
        return carry

    count = units[units.shape[0] - 1, LANES - 1]
    lax.fori_loop(0, (count + UNROLL - 1) // UNROLL, group, 0)

    total = sums[pl.ds(4, blocks, stride=32), :]
    forces = []
    for c in range(3):
        y = points[pl.ds(c * blocks, blocks), :]
        mix = (
            sums[pl.ds(c, blocks, stride=32), :]
            + sums[pl.ds(8 + c, blocks, stride=32), :]
            + sums[pl.ds(16 + c, blocks, stride=32), :]
        )
        forces.append((2.0 * STIFFNESS) * (y * total - mix))
    return forces


def build_units(size, shape, codes, out):
    devices, blocks = size
    nrow, ncol, span = shape
    row, col = lax.axis_index("row"), lax.axis_index("col")
    me = row * ncol + col
    shift = blocks.bit_length() - 1
    cshift = ncol.bit_length() - 1
    wide = (nrow * blocks).bit_length() - 1
    code = codes[...]
    height = code.shape[0]
    holder = lax.broadcasted_iota(jnp.int32, code.shape, 0) // span
    by_row = holder < ncol
    valid = (code >= 0) & (holder < ncol + nrow)
    left, right = code >> wide, code & (nrow * blocks - 1)
    left_owner = jnp.where(by_row, row, holder - ncol) * ncol + (left >> shift)
    right_owner = ((right >> shift) << cshift) + jnp.where(by_row, holder, col)
    left_place, right_place = left & (blocks - 1), right & (blocks - 1)
    distinct = (left_owner != right_owner) | (left_place != right_place)
    mine = jnp.where(by_row, left_place, right_place)
    owner = jnp.where(by_row, left_owner, right_owner)
    valid = valid & (owner == me) & (by_row | distinct)
    other = jnp.where(by_row, right_owner, left_owner)
    place = jnp.where(by_row, right_place, left_place)
    back = (devices - slot_of(other ^ me, devices)) * (4 * blocks) - place
    mine = jnp.where(valid, mine, -1)

    ones = jnp.bfloat16
    chosen = jnp.concatenate([(mine == b).astype(jnp.float32) for b in range(blocks)], 0)
    picked = chosen.astype(ones)
    one, two = lax.broadcasted_iota(jnp.int32, (LANES, LANES), 0), lax.broadcasted_iota(jnp.int32, (LANES, LANES), 1)
    before = matmul(picked, (one < two).astype(jnp.float32).astype(ones))
    totals = matmul(picked, jnp.ones((LANES, LANES), ones))
    many = blocks * height
    one, two = lax.broadcasted_iota(jnp.int32, (many, many), 0), lax.broadcasted_iota(jnp.int32, (many, many), 1)
    earlier = ((one // height == two // height) & (two < one)).astype(jnp.float32).astype(ones)
    above = matmul(earlier, totals.astype(ones))
    offset = jnp.zeros((1, LANES), jnp.float32)
    position = jnp.zeros(code.shape, jnp.float32)
    for b in range(blocks):
        part = slice(b * height, (b + 1) * height)
        position = position + chosen[part] * (before[part] + above[part] + offset)
        last = (b + 1) * height - 1
        filled = above[last : last + 1] + totals[last : last + 1]
        offset = offset + filled + (filled.astype(jnp.int32) & 1).astype(jnp.float32)
    position = position.astype(jnp.int32)
    high = jnp.where(valid, position >> 7, -1)
    low = position & (LANES - 1)

    rows = out.shape[0]
    pieces = [(back & 63).astype(jnp.float32), (back >> 6).astype(jnp.float32), mine.astype(jnp.float32)]
    lane = lax.broadcasted_iota(jnp.int32, (LANES, LANES), 0)
    place = lax.broadcasted_iota(jnp.int32, (rows, LANES), 0)
    found = jnp.zeros((3 * rows, LANES), jnp.float32)
    for r in range(height):
        here = high[r : r + 1] == place
        weights = jnp.concatenate([jnp.where(here, p[r : r + 1], 0.0) for p in pieces], 0)
        spots = (lane == low[r : r + 1]).astype(jnp.float32)
        found = found + lax.dot_general(
            weights.astype(ones), spots.astype(ones), (((1,), (1,)), ((), ())), preferred_element_type=jnp.float32
        )
    words = found.astype(jnp.int32)
    words = words[:rows] + words[rows : 2 * rows] * 64 + words[2 * rows :] * (BASE_MASK + 1)
    end = (place == rows - 1) & (lax.broadcasted_iota(jnp.int32, (rows, LANES), 1) == LANES - 1)
    out[...] = jnp.where(end, (offset * 0.5).astype(jnp.int32), words)


def first_kernel(size, shape, gathered, velocity, x_next, force_out, units, points, lefts, sums, codes, words, sem):
    devices, blocks = size
    nrow, ncol, span = shape
    rows = 3 * blocks + LIST_ROWS
    row, col = lax.axis_index("row"), lax.axis_index("col")
    me = row * ncol + col
    holders = [row * ncol + c for c in range(ncol)] + [r * ncol + col for r in range(nrow)]
    codes[...] = jnp.full_like(codes, -1)
    for n, holder in enumerate(holders):
        slot = slot_of(holder ^ me, devices)
        tile = gathered[pl.ds(pl.multiple_of(slot * rows + 3 * blocks, 8), LIST_ROWS), :]
        codes[pl.ds(n * span, span), :] = tile[:span].astype(jnp.int32)
    build_units(size, shape, codes, words)
    copy = pltpu.make_async_copy(words, units, sem)
    copy.start()
    copy.wait()
    forces = evaluate(size, gathered, rows, units, points, lefts, sums)
    for c in range(3):
        at = pl.ds(c * blocks, blocks)
        force_out[at, :] = forces[c]
        x_next[at, :] = gathered[at, :] + TIME_STEP * velocity[at, :] + (0.5 * TIME_STEP * TIME_STEP) * forces[c]


def next_kernel(size, last, gathered, velocity, force, units, x_next, v_next, *rest):
    devices, blocks = size
    if last:
        points, lefts, sums = rest
    else:
        force_out, points, lefts, sums = rest
    forces = evaluate(size, gathered, 3 * blocks, units, points, lefts, sums)
    for c in range(3):
        at = pl.ds(c * blocks, blocks)
        x = gathered[at, :]
        v = velocity[at, :] + (0.5 * TIME_STEP) * (force[at, :] + forces[c])
        v_next[at, :] = v
        if last:
            x_next[at, :] = x
        else:
            force_out[at, :] = forces[c]
            x_next[at, :] = x + TIME_STEP * v + (0.5 * TIME_STEP * TIME_STEP) * forces[c]


def body(positions, velocities, pair_lists, pair_counts):
    nrow, ncol = lax.axis_size("row"), lax.axis_size("col")
    devices = nrow * ncol
    blocks = positions.shape[1] // LANES
    pairs = pair_lists[0, 0]
    slots = pairs.shape[0]
    size = (devices, blocks)
    span = slots // LANES
    lists = pack_list(pairs, pair_counts[0, 0], nrow * blocks)
    entries = (nrow + ncol) * slots + blocks + 2 * UNROLL
    unit_rows = 8 * (entries // (8 * LANES) + 1)
    code_rows = 8 * (-(-(nrow + ncol) * span // 8))
    current = positions.reshape(3 * blocks, LANES)
    velocity = velocities.reshape(3 * blocks, LANES)

    flat = jax.ShapeDtypeStruct((3 * blocks, LANES), jnp.float32)
    unit_list = jax.ShapeDtypeStruct((unit_rows, LANES), jnp.int32)
    vmem = pl.BlockSpec(memory_space=pltpu.VMEM)
    smem = pl.BlockSpec(memory_space=pltpu.SMEM)
    scratch = [
        pltpu.VMEM(((devices + 3) * 4 * blocks, LANES), jnp.float32),
        pltpu.VMEM((blocks, 48, LANES), jnp.bfloat16),
        pltpu.VMEM((blocks * 32, LANES), jnp.float32),
    ]
    params = pltpu.CompilerParams(vmem_limit_bytes=48 * 1024 * 1024)

    gathered = gather(jnp.concatenate([current, lists], 0), devices)
    current, force, units = pl.pallas_call(
        functools.partial(first_kernel, size, (nrow, ncol, span)),
        out_shape=[flat, flat, unit_list],
        in_specs=[vmem, vmem],
        out_specs=[vmem, vmem, smem],
        scratch_shapes=scratch
        + [
            pltpu.VMEM((code_rows, LANES), jnp.int32),
            pltpu.VMEM((unit_rows, LANES), jnp.int32),
            pltpu.SemaphoreType.DMA,
        ],
        compiler_params=params,
        name="first_forces",
    )(gathered, velocity)
    for turn in range(STEPS):
        last = turn == STEPS - 1
        result = pl.pallas_call(
            functools.partial(next_kernel, size, last),
            out_shape=[flat] * (2 if last else 3),
            in_specs=[vmem, vmem, vmem, smem],
            out_specs=[vmem] * (2 if last else 3),
            scratch_shapes=scratch,
            compiler_params=params,
            name="last_forces" if last else "next_forces",
        )(gather(current, devices), velocity, force, units)
        if last:
            current, velocity = result
        else:
            current, velocity, force = result
    return current.reshape(positions.shape), velocity.reshape(velocities.shape)


def solution(mesh):
    placed = (
        P(None, ("row", "col")),
        P(None, ("row", "col")),
        P("row", "col", None, None),
        P("row", "col"),
    )
    return jax.shard_map(
        body,
        mesh=mesh,
        in_specs=placed,
        out_specs=(P(None, ("row", "col")), P(None, ("row", "col"))),
        check_vma=False,
    )
```

```python
import functools

import jax
import jax.numpy as jnp
from jax import lax
from jax.experimental import pallas as pl
from jax.experimental.pallas import tpu as pltpu
from jax.sharding import PartitionSpec as P

ATOM_DEV = 2048
PAIRS_MAX = 256
STEPS = 3
TIME_STEP = 0.5
STIFFNESS = ATOM_DEV / (2048.0 * PAIRS_MAX)

LANES = 128
LIST_ROWS = 8
UNROLL = 24
AHEAD = 6
BEHIND = 2
BASE_MASK = (1 << 14) - 1
FAR = 1.0e6
AXES = ("row", "col")


def stage_masks(devices):
    bits = devices.bit_length() - 1
    groups = [(0, 1)] if bits else []
    low = 1
    while low < bits:
        high = min(low + 2, bits)
        groups.append((low, high))
        low = high
    return [(lo, 1 << (hi - lo)) for lo, hi in reversed(groups)]


def gather(block, devices):
    for low, count in stage_masks(devices):
        parts = [block]
        for step in range(1, count):
            pairs = [(d, d ^ (step << low)) for d in range(devices)]
            parts.append(lax.ppermute(block, AXES, pairs))
        block = jnp.concatenate(parts, 0)
    return block


def slot_of(relative, devices):
    slot = jnp.zeros_like(relative)
    stride = 1
    for low, count in stage_masks(devices):
        slot = slot + ((relative >> low) & (count - 1)) * stride
        stride *= count
    return slot


def pack_list(pairs, total, span):
    valid = jnp.arange(pairs.shape[0], dtype=jnp.int32) < total
    code = jnp.where(valid, pairs[:, 0] * span + pairs[:, 1], -1).astype(jnp.float32)
    rows = code.reshape(-1, LANES)
    return jnp.pad(rows, ((0, LIST_ROWS - rows.shape[0]), (0, 0)))


def matmul(a, b):
    return jnp.dot(a, b, preferred_element_type=jnp.float32)


def split3(tile):
    high = tile.astype(jnp.bfloat16).astype(jnp.float32)
    rest = tile - high
    mid = rest.astype(jnp.bfloat16).astype(jnp.float32)
    return high, mid, rest - mid


def evaluate(size, gathered, rows, units, points, lefts, sums):
    devices, blocks = size
    stride = 4 * blocks
    dummy = devices * stride
    for slot in range(devices):
        norm = None
        for c in range(3):
            y = 0.5 * gathered[pl.ds(slot * rows + c * blocks, blocks), :]
            points[pl.ds(slot * stride + c * blocks, blocks), :] = y
            norm = y * y if norm is None else norm + y * y
        points[pl.ds(slot * stride + 3 * blocks, blocks), :] = norm
    points[pl.ds(dummy, 3 * blocks), :] = jnp.zeros((3 * blocks, LANES), jnp.float32)
    points[pl.ds(dummy + 3 * blocks, blocks), :] = jnp.full((blocks, LANES), FAR, jnp.float32)

    place = lax.broadcasted_iota(jnp.int32, (8, LANES), 0)
    for b in range(blocks):
        tile = points[pl.ds(b, 8, stride=blocks), :]
        moved = pltpu.roll(tile, 1, 0)
        tile = jnp.where(
            place < 3, 2.0 * tile, jnp.where(place == 3, -1.0, jnp.where(place == 4, 1.0 - moved, 0.0))
        )
        high, mid, low = split3(tile)
        lefts[b] = jnp.concatenate([high, high, high, mid, mid, low], 0).astype(jnp.bfloat16)
    sums[...] = jnp.zeros_like(sums)

    def right_tile(word):
        tile = points[pl.ds(dummy - (word & BASE_MASK), 8, stride=blocks), :]
        tile = jnp.where(place < 4, tile, jnp.where(place == 4, 1.0, 0.0))
        high, mid, low = split3(tile)
        return jnp.concatenate([high, mid, low, high, mid, high], 0).astype(jnp.bfloat16)

    def group(number, carry):
        def weigh(k):
            at = 2 * (number * UNROLL + k)
            words = [units[(at + n) // LANES, (at + n) % LANES] for n in range(2)]
            rights = [right_tile(word) for word in words]
            mine = words[0] // (BASE_MASK + 1)
            u = matmul(jnp.concatenate([r.T for r in rights], 0), lefts[mine])
            return mine, jnp.concatenate([r[:32] for r in rights], 1), u

        def halve(u):
            w = jnp.maximum(u, 0.0)
            high = w.astype(jnp.bfloat16)
            return jnp.concatenate([high, (w - high.astype(jnp.float32)).astype(jnp.bfloat16)], 1)

        def add(mine, right, w):
            part = matmul(right, w)
            at = pl.ds(pl.multiple_of(mine * 32, 32), 32)
            sums[at, :] = sums[at, :] + (part[:, :LANES] + part[:, LANES:])

        staged, halved = [], []
        for k in range(UNROLL + AHEAD + BEHIND):
            if k < UNROLL:
                staged.append(weigh(k))
            if 0 <= k - AHEAD < UNROLL:
                halved.append(halve(staged[k - AHEAD][2]))
            if k >= AHEAD + BEHIND:
                mine, right, _ = staged[k - AHEAD - BEHIND]
                add(mine, right, halved[k - AHEAD - BEHIND])
        return carry

    count = units[units.shape[0] - 1, LANES - 1]
    lax.fori_loop(0, (count + UNROLL - 1) // UNROLL, group, 0)

    total = sums[pl.ds(4, blocks, stride=32), :]
    forces = []
    for c in range(3):
        y = points[pl.ds(c * blocks, blocks), :]
        mix = (
            sums[pl.ds(c, blocks, stride=32), :]
            + sums[pl.ds(8 + c, blocks, stride=32), :]
            + sums[pl.ds(16 + c, blocks, stride=32), :]
        )
        forces.append((2.0 * STIFFNESS) * (y * total - mix))
    return forces


def build_units(size, shape, codes, out):
    devices, blocks = size
    nrow, ncol, span = shape
    row, col = lax.axis_index("row"), lax.axis_index("col")
    me = row * ncol + col
    shift = blocks.bit_length() - 1
    cshift = ncol.bit_length() - 1
    wide = (nrow * blocks).bit_length() - 1
    code = codes[...]
    height = code.shape[0]
    holder = lax.broadcasted_iota(jnp.int32, code.shape, 0) // span
    by_row = holder < ncol
    valid = (code >= 0) & (holder < ncol + nrow)
    left, right = code >> wide, code & (nrow * blocks - 1)
    left_owner = jnp.where(by_row, row, holder - ncol) * ncol + (left >> shift)
    right_owner = ((right >> shift) << cshift) + jnp.where(by_row, holder, col)
    left_place, right_place = left & (blocks - 1), right & (blocks - 1)
    distinct = (left_owner != right_owner) | (left_place != right_place)
    mine = jnp.where(by_row, left_place, right_place)
    owner = jnp.where(by_row, left_owner, right_owner)
    valid = valid & (owner == me) & (by_row | distinct)
    other = jnp.where(by_row, right_owner, left_owner)
    place = jnp.where(by_row, right_place, left_place)
    back = (devices - slot_of(other ^ me, devices)) * (4 * blocks) - place
    mine = jnp.where(valid, mine, -1)

    ones = jnp.bfloat16
    chosen = jnp.concatenate([(mine == b).astype(jnp.float32) for b in range(blocks)], 0)
    picked = chosen.astype(ones)
    one, two = lax.broadcasted_iota(jnp.int32, (LANES, LANES), 0), lax.broadcasted_iota(jnp.int32, (LANES, LANES), 1)
    before = matmul(picked, (one < two).astype(jnp.float32).astype(ones))
    totals = matmul(picked, jnp.ones((LANES, LANES), ones))
    many = blocks * height
    one, two = lax.broadcasted_iota(jnp.int32, (many, many), 0), lax.broadcasted_iota(jnp.int32, (many, many), 1)
    earlier = ((one // height == two // height) & (two < one)).astype(jnp.float32).astype(ones)
    above = matmul(earlier, totals.astype(ones))
    offset = jnp.zeros((1, LANES), jnp.float32)
    position = jnp.zeros(code.shape, jnp.float32)
    for b in range(blocks):
        part = slice(b * height, (b + 1) * height)
        position = position + chosen[part] * (before[part] + above[part] + offset)
        last = (b + 1) * height - 1
        filled = above[last : last + 1] + totals[last : last + 1]
        offset = offset + filled + (filled.astype(jnp.int32) & 1).astype(jnp.float32)
    position = position.astype(jnp.int32)
    high = jnp.where(valid, position >> 7, -1)
    low = position & (LANES - 1)

    rows = out.shape[0]
    pieces = [(back & 63).astype(jnp.float32), (back >> 6).astype(jnp.float32), mine.astype(jnp.float32)]
    lane = lax.broadcasted_iota(jnp.int32, (LANES, LANES), 0)
    place = lax.broadcasted_iota(jnp.int32, (rows, LANES), 0)
    found = jnp.zeros((3 * rows, LANES), jnp.float32)
    for r in range(height):
        here = high[r : r + 1] == place
        weights = jnp.concatenate([jnp.where(here, p[r : r + 1], 0.0) for p in pieces], 0)
        spots = (lane == low[r : r + 1]).astype(jnp.float32)
        found = found + lax.dot_general(
            weights.astype(ones), spots.astype(ones), (((1,), (1,)), ((), ())), preferred_element_type=jnp.float32
        )
    words = found.astype(jnp.int32)
    words = words[:rows] + words[rows : 2 * rows] * 64 + words[2 * rows :] * (BASE_MASK + 1)
    end = (place == rows - 1) & (lax.broadcasted_iota(jnp.int32, (rows, LANES), 1) == LANES - 1)
    out[...] = jnp.where(end, (offset * 0.5).astype(jnp.int32), words)


def first_kernel(size, shape, gathered, velocity, x_next, force_out, units, points, lefts, sums, codes, words, sem):
    devices, blocks = size
    nrow, ncol, span = shape
    rows = 3 * blocks + LIST_ROWS
    row, col = lax.axis_index("row"), lax.axis_index("col")
    me = row * ncol + col
    holders = [row * ncol + c for c in range(ncol)] + [r * ncol + col for r in range(nrow)]
    codes[...] = jnp.full_like(codes, -1)
    for n, holder in enumerate(holders):
        slot = slot_of(holder ^ me, devices)
        tile = gathered[pl.ds(pl.multiple_of(slot * rows + 3 * blocks, 8), LIST_ROWS), :]
        codes[pl.ds(n * span, span), :] = tile[:span].astype(jnp.int32)
    build_units(size, shape, codes, words)
    copy = pltpu.make_async_copy(words, units, sem)
    copy.start()
    copy.wait()
    forces = evaluate(size, gathered, rows, units, points, lefts, sums)
    for c in range(3):
        at = pl.ds(c * blocks, blocks)
        force_out[at, :] = forces[c]
        x_next[at, :] = gathered[at, :] + TIME_STEP * velocity[at, :] + (0.5 * TIME_STEP * TIME_STEP) * forces[c]


def next_kernel(size, last, gathered, velocity, force, units, x_next, v_next, *rest):
    devices, blocks = size
    if last:
        points, lefts, sums = rest
    else:
        force_out, points, lefts, sums = rest
    forces = evaluate(size, gathered, 3 * blocks, units, points, lefts, sums)
    for c in range(3):
        at = pl.ds(c * blocks, blocks)
        x = gathered[at, :]
        v = velocity[at, :] + (0.5 * TIME_STEP) * (force[at, :] + forces[c])
        v_next[at, :] = v
        if last:
            x_next[at, :] = x
        else:
            force_out[at, :] = forces[c]
            x_next[at, :] = x + TIME_STEP * v + (0.5 * TIME_STEP * TIME_STEP) * forces[c]


def body(positions, velocities, pair_lists, pair_counts):
    nrow, ncol = lax.axis_size("row"), lax.axis_size("col")
    devices = nrow * ncol
    blocks = positions.shape[1] // LANES
    pairs = pair_lists[0, 0]
    slots = pairs.shape[0]
    size = (devices, blocks)
    span = slots // LANES
    lists = pack_list(pairs, pair_counts[0, 0], nrow * blocks)
    entries = (nrow + ncol) * slots + blocks + 2 * UNROLL
    unit_rows = 8 * (entries // (8 * LANES) + 1)
    code_rows = 8 * (-(-(nrow + ncol) * span // 8))
    current = positions.reshape(3 * blocks, LANES)
    velocity = velocities.reshape(3 * blocks, LANES)

    flat = jax.ShapeDtypeStruct((3 * blocks, LANES), jnp.float32)
    unit_list = jax.ShapeDtypeStruct((unit_rows, LANES), jnp.int32)
    vmem = pl.BlockSpec(memory_space=pltpu.VMEM)
    smem = pl.BlockSpec(memory_space=pltpu.SMEM)
    scratch = [
        pltpu.VMEM(((devices + 3) * 4 * blocks, LANES), jnp.float32),
        pltpu.VMEM((blocks, 48, LANES), jnp.bfloat16),
        pltpu.VMEM((blocks * 32, LANES), jnp.float32),
    ]
    params = pltpu.CompilerParams(vmem_limit_bytes=48 * 1024 * 1024)

    gathered = gather(jnp.concatenate([current, lists], 0), devices)
    current, force, units = pl.pallas_call(
        functools.partial(first_kernel, size, (nrow, ncol, span)),
        out_shape=[flat, flat, unit_list],
        in_specs=[vmem, vmem],
        out_specs=[vmem, vmem, smem],
        scratch_shapes=scratch
        + [
            pltpu.VMEM((code_rows, LANES), jnp.int32),
            pltpu.VMEM((unit_rows, LANES), jnp.int32),
            pltpu.SemaphoreType.DMA,
        ],
        compiler_params=params,
        name="first_forces",
    )(gathered, velocity)
    for turn in range(STEPS):
        last = turn == STEPS - 1
        result = pl.pallas_call(
            functools.partial(next_kernel, size, last),
            out_shape=[flat] * (2 if last else 3),
            in_specs=[vmem, vmem, vmem, smem],
            out_specs=[vmem] * (2 if last else 3),
            scratch_shapes=scratch,
            compiler_params=params,
            name="last_forces" if last else "next_forces",
        )(gather(current, devices), velocity, force, units)
        if last:
            current, velocity = result
        else:
            current, velocity, force = result
    return current.reshape(positions.shape), velocity.reshape(velocities.shape)


def solution(mesh):
    placed = (
        P(None, ("row", "col")),
        P(None, ("row", "col")),
        P("row", "col", None, None),
        P("row", "col"),
    )
    return jax.shard_map(
        body,
        mesh=mesh,
        in_specs=placed,
        out_specs=(P(None, ("row", "col")), P(None, ("row", "col"))),
        check_vma=False,
    )
```

```python
import functools

import jax
import jax.numpy as jnp
from jax import lax
from jax.experimental import pallas as pl
from jax.experimental.pallas import tpu as pltpu
from jax.sharding import PartitionSpec as P

ATOM_DEV = 2048
PAIRS_MAX = 256
STEPS = 3
TIME_STEP = 0.5
STIFFNESS = ATOM_DEV / (2048.0 * PAIRS_MAX)

LANES = 128
LIST_ROWS = 8
UNROLL = 32
LEAD = 4
LAG = 8
BASE_BITS = 14
BASE_MASK = (1 << BASE_BITS) - 1
FAR = 1.0e6
AXES = ("row", "col")


def stage_masks(devices):
    bits = devices.bit_length() - 1
    groups = [(0, 1)] if bits else []
    low = 1
    while low < bits:
        high = min(low + 2, bits)
        groups.append((low, high))
        low = high
    return [(lo, 1 << (hi - lo)) for lo, hi in reversed(groups)]


def gather(block, devices):
    for low, count in stage_masks(devices):
        parts = [block]
        for step in range(1, count):
            pairs = [(d, d ^ (step << low)) for d in range(devices)]
            parts.append(lax.ppermute(block, AXES, pairs))
        block = jnp.concatenate(parts, 0)
    return block


def slot_of(relative, devices):
    slot = jnp.zeros_like(relative)
    stride = 1
    for low, count in stage_masks(devices):
        slot = slot + ((relative >> low) & (count - 1)) * stride
        stride *= count
    return slot


def pack_list(pairs, total, span):
    valid = jnp.arange(pairs.shape[0], dtype=jnp.int32) < total
    code = jnp.where(valid, pairs[:, 0] * span + pairs[:, 1], -1).astype(jnp.float32)
    rows = code.reshape(-1, LANES)
    return jnp.pad(rows, ((0, LIST_ROWS - rows.shape[0]), (0, 0)))


def matmul(a, b):
    return jnp.dot(a, b, preferred_element_type=jnp.float32)


def split3(tile):
    high = tile.astype(jnp.bfloat16).astype(jnp.float32)
    rest = tile - high
    mid = rest.astype(jnp.bfloat16).astype(jnp.float32)
    return high, mid, rest - mid


def evaluate(size, gathered, rows, units, points, lefts, sums, turned_kept, right_kept, weights_kept, partner_kept):
    devices, blocks = size
    stride = 4 * blocks
    dummy = devices * stride
    for slot in range(devices):
        norm = None
        for c in range(3):
            y = 0.5 * gathered[pl.ds(slot * rows + c * blocks, blocks), :]
            points[pl.ds(slot * stride + c * blocks, blocks), :] = y
            norm = y * y if norm is None else norm + y * y
        points[pl.ds(slot * stride + 3 * blocks, blocks), :] = norm
    points[pl.ds(dummy, 3 * blocks), :] = jnp.zeros((3 * blocks, LANES), jnp.float32)
    points[pl.ds(dummy + 3 * blocks, blocks), :] = jnp.full((blocks, LANES), FAR, jnp.float32)

    place = lax.broadcasted_iota(jnp.int32, (8, LANES), 0)
    for b in range(blocks):
        tile = points[pl.ds(b, 8, stride=blocks), :]
        moved = pltpu.roll(tile, 1, 0)
        tile = jnp.where(
            place < 3, 2.0 * tile, jnp.where(place == 3, -1.0, jnp.where(place == 4, 1.0 - moved, 0.0))
        )
        high, mid, low = split3(tile)
        lefts[b] = jnp.concatenate([high, high, high, mid, mid, low], 0).astype(jnp.bfloat16)
    sums[...] = jnp.zeros_like(sums)

    def right_tile(word):
        tile = points[pl.ds(dummy - (word & BASE_MASK), 8, stride=blocks), :]
        tile = jnp.where(place < 4, tile, jnp.where(place == 4, 1.0, 0.0))
        high, mid, low = split3(tile)
        return jnp.concatenate([high, mid, low, high, mid, high], 0).astype(jnp.bfloat16)

    def word(unit, n):
        at = 2 * unit + n
        return units[at >> 7, at & (LANES - 1)]

    def block_of(unit):
        return word(unit, 0) >> BASE_BITS

    def fetch(unit):
        rights = [right_tile(word(unit, n)) for n in range(2)]
        return jnp.concatenate([r.T for r in rights], 0), jnp.concatenate([r[:32] for r in rights], 1)

    def weigh(unit, turned):
        w = jnp.maximum(matmul(turned, lefts[block_of(unit)]), 0.0)
        high = w.astype(jnp.bfloat16)
        return jnp.concatenate([high, (w - high.astype(jnp.float32)).astype(jnp.bfloat16)], 1)

    def add(unit, right, w):
        part = matmul(right, w)
        at = pl.ds(pl.multiple_of(block_of(unit) * 32, 32), 32)
        sums[at, :] = sums[at, :] + (part[:, :LANES] + part[:, LANES:])

    for k in range(LEAD):
        turned_kept[k], right_kept[k] = fetch(k)
    weights_kept[...] = jnp.zeros_like(weights_kept)
    partner_kept[...] = jnp.zeros_like(partner_kept)

    def group(number, carry):
        first = number * UNROLL
        fetched = [(turned_kept[k], right_kept[k]) for k in range(LEAD)]
        weighed = [(partner_kept[k], weights_kept[k]) for k in range(LAG)]
        for k in range(UNROLL):
            add(jnp.maximum(first + k - LAG, 0), *weighed[k])
            turned, right = fetched[k]
            weighed.append((right, weigh(first + k, turned)))
            fetched.append(fetch(first + k + LEAD))
        for k in range(LEAD):
            turned_kept[k], right_kept[k] = fetched[UNROLL + k]
        for k in range(LAG):
            partner_kept[k], weights_kept[k] = weighed[UNROLL + k]
        return carry

    count = units[units.shape[0] - 1, LANES - 1]
    steps = (count + UNROLL - 1) >> (UNROLL.bit_length() - 1)
    lax.fori_loop(0, steps, group, 0)
    for k in range(LAG):
        add(jnp.maximum(steps * UNROLL - LAG + k, 0), partner_kept[k], weights_kept[k])

    total = sums[pl.ds(4, blocks, stride=32), :]
    forces = []
    for c in range(3):
        y = points[pl.ds(c * blocks, blocks), :]
        mix = (
            sums[pl.ds(c, blocks, stride=32), :]
            + sums[pl.ds(8 + c, blocks, stride=32), :]
            + sums[pl.ds(16 + c, blocks, stride=32), :]
        )
        forces.append((2.0 * STIFFNESS) * (y * total - mix))
    return forces


def build_units(size, shape, codes, out):
    devices, blocks = size
    nrow, ncol, span = shape
    row, col = lax.axis_index("row"), lax.axis_index("col")
    me = row * ncol + col
    shift = blocks.bit_length() - 1
    cshift = ncol.bit_length() - 1
    wide = (nrow * blocks).bit_length() - 1
    code = codes[...]
    height = code.shape[0]
    holder = lax.broadcasted_iota(jnp.int32, code.shape, 0) // span
    by_row = holder < ncol
    valid = (code >= 0) & (holder < ncol + nrow)
    left, right = code >> wide, code & (nrow * blocks - 1)
    left_owner = jnp.where(by_row, row, holder - ncol) * ncol + (left >> shift)
    right_owner = ((right >> shift) << cshift) + jnp.where(by_row, holder, col)
    left_place, right_place = left & (blocks - 1), right & (blocks - 1)
    distinct = (left_owner != right_owner) | (left_place != right_place)
    mine = jnp.where(by_row, left_place, right_place)
    owner = jnp.where(by_row, left_owner, right_owner)
    valid = valid & (owner == me) & (by_row | distinct)
    other = jnp.where(by_row, right_owner, left_owner)
    place = jnp.where(by_row, right_place, left_place)
    back = (devices - slot_of(other ^ me, devices)) * (4 * blocks) - place
    mine = jnp.where(valid, mine, -1)

    ones = jnp.bfloat16
    chosen = jnp.concatenate([(mine == b).astype(jnp.float32) for b in range(blocks)], 0)
    picked = chosen.astype(ones)
    one, two = lax.broadcasted_iota(jnp.int32, (LANES, LANES), 0), lax.broadcasted_iota(jnp.int32, (LANES, LANES), 1)
    before = matmul(picked, (one < two).astype(jnp.float32).astype(ones))
    totals = matmul(picked, jnp.ones((LANES, LANES), ones))
    many = blocks * height
    one, two = lax.broadcasted_iota(jnp.int32, (many, many), 0), lax.broadcasted_iota(jnp.int32, (many, many), 1)
    earlier = ((one // height == two // height) & (two < one)).astype(jnp.float32).astype(ones)
    above = matmul(earlier, totals.astype(ones))
    offset = jnp.zeros((1, LANES), jnp.float32)
    position = jnp.zeros(code.shape, jnp.float32)
    for b in range(blocks):
        part = slice(b * height, (b + 1) * height)
        position = position + chosen[part] * (before[part] + above[part] + offset)
        last = (b + 1) * height - 1
        filled = above[last : last + 1] + totals[last : last + 1]
        offset = offset + filled + (filled.astype(jnp.int32) & 1).astype(jnp.float32)
    position = position.astype(jnp.int32)
    high = jnp.where(valid, position >> 7, -1)
    low = position & (LANES - 1)

    rows = out.shape[0]
    pieces = [(back & 63).astype(jnp.float32), (back >> 6).astype(jnp.float32), mine.astype(jnp.float32)]
    lane = lax.broadcasted_iota(jnp.int32, (LANES, LANES), 0)
    place = lax.broadcasted_iota(jnp.int32, (rows, LANES), 0)
    found = jnp.zeros((3 * rows, LANES), jnp.float32)
    for r in range(height):
        here = high[r : r + 1] == place
        weights = jnp.concatenate([jnp.where(here, p[r : r + 1], 0.0) for p in pieces], 0)
        spots = (lane == low[r : r + 1]).astype(jnp.float32)
        found = found + lax.dot_general(
            weights.astype(ones), spots.astype(ones), (((1,), (1,)), ((), ())), preferred_element_type=jnp.float32
        )
    words = found.astype(jnp.int32)
    words = words[:rows] + words[rows : 2 * rows] * 64 + words[2 * rows :] * (BASE_MASK + 1)
    end = (place == rows - 1) & (lax.broadcasted_iota(jnp.int32, (rows, LANES), 1) == LANES - 1)
    out[...] = jnp.where(end, (offset * 0.5).astype(jnp.int32), words)


def first_kernel(size, shape, gathered, velocity, x_next, force_out, units, codes, words, sem, *scratch):
    devices, blocks = size
    nrow, ncol, span = shape
    rows = 3 * blocks + LIST_ROWS
    row, col = lax.axis_index("row"), lax.axis_index("col")
    me = row * ncol + col
    holders = [row * ncol + c for c in range(ncol)] + [r * ncol + col for r in range(nrow)]
    codes[...] = jnp.full_like(codes, -1)
    for n, holder in enumerate(holders):
        slot = slot_of(holder ^ me, devices)
        tile = gathered[pl.ds(pl.multiple_of(slot * rows + 3 * blocks, 8), LIST_ROWS), :]
        codes[pl.ds(n * span, span), :] = tile[:span].astype(jnp.int32)
    build_units(size, shape, codes, words)
    copy = pltpu.make_async_copy(words, units, sem)
    copy.start()
    copy.wait()
    forces = evaluate(size, gathered, rows, units, *scratch)
    for c in range(3):
        at = pl.ds(c * blocks, blocks)
        force_out[at, :] = forces[c]
        x_next[at, :] = gathered[at, :] + TIME_STEP * velocity[at, :] + (0.5 * TIME_STEP * TIME_STEP) * forces[c]


def next_kernel(size, last, gathered, velocity, force, units, x_next, v_next, *rest):
    devices, blocks = size
    if last:
        scratch = rest
    else:
        force_out, *scratch = rest
    forces = evaluate(size, gathered, 3 * blocks, units, *scratch)
    for c in range(3):
        at = pl.ds(c * blocks, blocks)
        x = gathered[at, :]
        v = velocity[at, :] + (0.5 * TIME_STEP) * (force[at, :] + forces[c])
        v_next[at, :] = v
        if last:
            x_next[at, :] = x
        else:
            force_out[at, :] = forces[c]
            x_next[at, :] = x + TIME_STEP * v + (0.5 * TIME_STEP * TIME_STEP) * forces[c]


def body(positions, velocities, pair_lists, pair_counts):
    nrow, ncol = lax.axis_size("row"), lax.axis_size("col")
    devices = nrow * ncol
    blocks = positions.shape[1] // LANES
    pairs = pair_lists[0, 0]
    slots = pairs.shape[0]
    size = (devices, blocks)
    span = slots // LANES
    lists = pack_list(pairs, pair_counts[0, 0], nrow * blocks)
    entries = (nrow + ncol) * slots + blocks + 2 * (UNROLL + LEAD)
    unit_rows = 8 * (entries // (8 * LANES) + 1)
    code_rows = 8 * (-(-(nrow + ncol) * span // 8))
    current = positions.reshape(3 * blocks, LANES)
    velocity = velocities.reshape(3 * blocks, LANES)

    flat = jax.ShapeDtypeStruct((3 * blocks, LANES), jnp.float32)
    unit_list = jax.ShapeDtypeStruct((unit_rows, LANES), jnp.int32)
    vmem = pl.BlockSpec(memory_space=pltpu.VMEM)
    smem = pl.BlockSpec(memory_space=pltpu.SMEM)
    scratch = [
        pltpu.VMEM(((devices + 3) * 4 * blocks, LANES), jnp.float32),
        pltpu.VMEM((blocks, 48, LANES), jnp.bfloat16),
        pltpu.VMEM((blocks * 32, LANES), jnp.float32),
        pltpu.VMEM((LEAD, 2 * LANES, 48), jnp.bfloat16),
        pltpu.VMEM((LEAD, 32, 2 * LANES), jnp.bfloat16),
        pltpu.VMEM((LAG, 2 * LANES, 2 * LANES), jnp.bfloat16),
        pltpu.VMEM((LAG, 32, 2 * LANES), jnp.bfloat16),
    ]
    params = pltpu.CompilerParams(vmem_limit_bytes=48 * 1024 * 1024)

    gathered = gather(jnp.concatenate([current, lists], 0), devices)
    current, force, units = pl.pallas_call(
        functools.partial(first_kernel, size, (nrow, ncol, span)),
        out_shape=[flat, flat, unit_list],
        in_specs=[vmem, vmem],
        out_specs=[vmem, vmem, smem],
        scratch_shapes=[
            pltpu.VMEM((code_rows, LANES), jnp.int32),
            pltpu.VMEM((unit_rows, LANES), jnp.int32),
            pltpu.SemaphoreType.DMA,
        ]
        + scratch,
        compiler_params=params,
        name="first_forces",
    )(gathered, velocity)
    for turn in range(STEPS):
        last = turn == STEPS - 1
        result = pl.pallas_call(
            functools.partial(next_kernel, size, last),
            out_shape=[flat] * (2 if last else 3),
            in_specs=[vmem, vmem, vmem, smem],
            out_specs=[vmem] * (2 if last else 3),
            scratch_shapes=scratch,
            compiler_params=params,
            name="last_forces" if last else "next_forces",
        )(gather(current, devices), velocity, force, units)
        if last:
            current, velocity = result
        else:
            current, velocity, force = result
    return current.reshape(positions.shape), velocity.reshape(velocities.shape)


def solution(mesh):
    placed = (
        P(None, ("row", "col")),
        P(None, ("row", "col")),
        P("row", "col", None, None),
        P("row", "col"),
    )
    return jax.shard_map(
        body,
        mesh=mesh,
        in_specs=placed,
        out_specs=(P(None, ("row", "col")), P(None, ("row", "col"))),
        check_vma=False,
    )
```

```python
import functools

import jax
import jax.numpy as jnp
from jax import lax
from jax.experimental import pallas as pl
from jax.experimental.pallas import tpu as pltpu
from jax.sharding import PartitionSpec as P

ATOM_DEV = 2048
PAIRS_MAX = 256
STEPS = 3
TIME_STEP = 0.5
STIFFNESS = ATOM_DEV / (2048.0 * PAIRS_MAX)

LANES = 128
LIST_ROWS = 8
UNROLL = 32
LEAD = 4
LAG = 8
BASE_BITS = 14
BASE_MASK = (1 << BASE_BITS) - 1
FAR = 1.0e6
AXES = ("row", "col")


def stage_masks(devices):
    bits = devices.bit_length() - 1
    groups = [(0, 1)] if bits else []
    low = 1
    while low < bits:
        high = min(low + 2, bits)
        groups.append((low, high))
        low = high
    return [(lo, 1 << (hi - lo)) for lo, hi in reversed(groups)]


def send(block, devices, mask):
    return lax.ppermute(block, AXES, [(d, d ^ mask(d)) for d in range(devices)])


def gather(block, devices):
    stages = stage_masks(devices)[:-1]
    near, far, missing = block, None, [block]
    for number, (low, count) in enumerate(stages):
        if number == 0 and count == 4:
            far = send(block, devices, lambda d: 1)
            both = jnp.concatenate([near, far], 0)
            third = send(near, devices, lambda d: 3 << low)
            whole = send(both, devices, lambda d: (1 + d % 2) << low)
            missing = [whole, third]
            near = jnp.concatenate([near] + missing, 0)
        else:
            parts = [send(near, devices, lambda d: step << low) for step in range(1, count)]
            missing = missing + parts
            near = jnp.concatenate([near] + parts, 0)
    rest = send(jnp.concatenate(missing, 0), devices, lambda d: 1)
    return jnp.concatenate([near, rest] if far is None else [near, far, rest], 0)


def slot_of(owner, me, devices):
    relative = owner ^ me
    holder = owner & 1
    place = jnp.zeros_like(relative)
    size = 1
    for number, (low, count) in enumerate(stage_masks(devices)[:-1]):
        step = (relative >> low) & (count - 1)
        if number == 0 and count == 4:
            fetcher = jnp.where((step == 1) | (step == 2), step - 1, holder)
            place = jnp.where(step == 0, place, jnp.where(step == 3, 3, 1 + (holder ^ fetcher)))
            holder = fetcher
        else:
            place = place + step * size
        size *= count
    return place + (holder ^ (me & 1)) * size


def prepare_kernel(blocks, span, positions, velocities, pairs, total, out, velocity):
    slots = pairs.shape[1]
    for c in range(3):
        for b in range(blocks):
            at, lanes = pl.ds(c * blocks + b, 1), pl.ds(b * LANES, LANES)
            out[at, :] = positions[pl.ds(c, 1), lanes]
            velocity[at, :] = velocities[pl.ds(c, 1), lanes]
    live = lax.broadcasted_iota(jnp.int32, (1, slots), 1) < total[0, 0]
    code = jnp.where(live, pairs[0:1, :] * span + pairs[1:2, :], -1).astype(jnp.float32)
    out[pl.ds(3 * blocks, LIST_ROWS), :] = jnp.zeros((LIST_ROWS, LANES), jnp.float32)
    for r in range(slots // LANES):
        out[pl.ds(3 * blocks + r, 1), :] = code[:, r * LANES : (r + 1) * LANES]


def matmul(a, b):
    return jnp.dot(a, b, preferred_element_type=jnp.float32)


def split3(tile):
    high = tile.astype(jnp.bfloat16).astype(jnp.float32)
    rest = tile - high
    mid = rest.astype(jnp.bfloat16).astype(jnp.float32)
    return high, mid, rest - mid


def evaluate(size, gathered, rows, units, points, lefts, sums, turned_kept, right_kept, weights_kept, partner_kept):
    devices, blocks = size
    stride = 4 * blocks
    dummy = devices * stride
    for slot in range(devices):
        norm = None
        for c in range(3):
            y = 0.5 * gathered[pl.ds(slot * rows + c * blocks, blocks), :]
            points[pl.ds(slot * stride + c * blocks, blocks), :] = y
            norm = y * y if norm is None else norm + y * y
        points[pl.ds(slot * stride + 3 * blocks, blocks), :] = norm
    points[pl.ds(dummy, 3 * blocks), :] = jnp.zeros((3 * blocks, LANES), jnp.float32)
    points[pl.ds(dummy + 3 * blocks, blocks), :] = jnp.full((blocks, LANES), FAR, jnp.float32)

    place = lax.broadcasted_iota(jnp.int32, (8, LANES), 0)
    for b in range(blocks):
        tile = points[pl.ds(b, 8, stride=blocks), :]
        moved = pltpu.roll(tile, 1, 0)
        tile = jnp.where(
            place < 3, 2.0 * tile, jnp.where(place == 3, -1.0, jnp.where(place == 4, 1.0 - moved, 0.0))
        )
        high, mid, low = split3(tile)
        lefts[b] = jnp.concatenate([high, high, high, mid, mid, low], 0).astype(jnp.bfloat16)
    sums[...] = jnp.zeros_like(sums)

    def right_tile(word):
        tile = points[pl.ds(dummy - (word & BASE_MASK), 8, stride=blocks), :]
        tile = jnp.where(place < 4, tile, jnp.where(place == 4, 1.0, 0.0))
        high, mid, low = split3(tile)
        return jnp.concatenate([high, mid, low, high, mid, high], 0).astype(jnp.bfloat16)

    def word(unit, n):
        at = 2 * unit + n
        return units[at >> 7, at & (LANES - 1)]

    def block_of(unit):
        return word(unit, 0) >> BASE_BITS

    def fetch(unit):
        rights = [right_tile(word(unit, n)) for n in range(2)]
        return jnp.concatenate([r.T for r in rights], 0), jnp.concatenate([r[:32] for r in rights], 1)

    def weigh(unit, turned):
        w = jnp.maximum(matmul(turned, lefts[block_of(unit)]), 0.0)
        high = w.astype(jnp.bfloat16)
        return jnp.concatenate([high, (w - high.astype(jnp.float32)).astype(jnp.bfloat16)], 1)

    def add(unit, right, w):
        part = matmul(right, w)
        at = pl.ds(pl.multiple_of(block_of(unit) * 32, 32), 32)
        sums[at, :] = sums[at, :] + (part[:, :LANES] + part[:, LANES:])

    for k in range(LEAD):
        turned_kept[k], right_kept[k] = fetch(k)
    weights_kept[...] = jnp.zeros_like(weights_kept)
    partner_kept[...] = jnp.zeros_like(partner_kept)

    def group(number, carry):
        first = number * UNROLL
        fetched = [(turned_kept[k], right_kept[k]) for k in range(LEAD)]
        weighed = [(partner_kept[k], weights_kept[k]) for k in range(LAG)]
        for k in range(UNROLL):
            add(jnp.maximum(first + k - LAG, 0), *weighed[k])
            turned, right = fetched[k]
            weighed.append((right, weigh(first + k, turned)))
            fetched.append(fetch(first + k + LEAD))
        for k in range(LEAD):
            turned_kept[k], right_kept[k] = fetched[UNROLL + k]
        for k in range(LAG):
            partner_kept[k], weights_kept[k] = weighed[UNROLL + k]
        return carry

    count = units[units.shape[0] - 1, LANES - 1]
    steps = (count + UNROLL - 1) >> (UNROLL.bit_length() - 1)
    lax.fori_loop(0, steps, group, 0)
    for k in range(LAG):
        add(jnp.maximum(steps * UNROLL - LAG + k, 0), partner_kept[k], weights_kept[k])

    total = sums[pl.ds(4, blocks, stride=32), :]
    forces = []
    for c in range(3):
        y = points[pl.ds(c * blocks, blocks), :]
        mix = (
            sums[pl.ds(c, blocks, stride=32), :]
            + sums[pl.ds(8 + c, blocks, stride=32), :]
            + sums[pl.ds(16 + c, blocks, stride=32), :]
        )
        forces.append((2.0 * STIFFNESS) * (y * total - mix))
    return forces


def build_units(size, shape, codes, out):
    devices, blocks = size
    nrow, ncol, span = shape
    row, col = lax.axis_index("row"), lax.axis_index("col")
    me = row * ncol + col
    shift = blocks.bit_length() - 1
    cshift = ncol.bit_length() - 1
    wide = (nrow * blocks).bit_length() - 1
    code = codes[...]
    height = code.shape[0]
    holder = lax.broadcasted_iota(jnp.int32, code.shape, 0) // span
    by_row = holder < ncol
    valid = (code >= 0) & (holder < ncol + nrow)
    left, right = code >> wide, code & (nrow * blocks - 1)
    left_owner = jnp.where(by_row, row, holder - ncol) * ncol + (left >> shift)
    right_owner = ((right >> shift) << cshift) + jnp.where(by_row, holder, col)
    left_place, right_place = left & (blocks - 1), right & (blocks - 1)
    distinct = (left_owner != right_owner) | (left_place != right_place)
    mine = jnp.where(by_row, left_place, right_place)
    owner = jnp.where(by_row, left_owner, right_owner)
    valid = valid & (owner == me) & (by_row | distinct)
    other = jnp.where(by_row, right_owner, left_owner)
    place = jnp.where(by_row, right_place, left_place)
    back = (devices - slot_of(other, me, devices)) * (4 * blocks) - place
    mine = jnp.where(valid, mine, -1)

    ones = jnp.bfloat16
    chosen = jnp.concatenate([(mine == b).astype(jnp.float32) for b in range(blocks)], 0)
    picked = chosen.astype(ones)
    one, two = lax.broadcasted_iota(jnp.int32, (LANES, LANES), 0), lax.broadcasted_iota(jnp.int32, (LANES, LANES), 1)
    before = matmul(picked, (one < two).astype(jnp.float32).astype(ones))
    totals = matmul(picked, jnp.ones((LANES, LANES), ones))
    many = blocks * height
    one, two = lax.broadcasted_iota(jnp.int32, (many, many), 0), lax.broadcasted_iota(jnp.int32, (many, many), 1)
    earlier = ((one // height == two // height) & (two < one)).astype(jnp.float32).astype(ones)
    above = matmul(earlier, totals.astype(ones))
    offset = jnp.zeros((1, LANES), jnp.float32)
    position = jnp.zeros(code.shape, jnp.float32)
    for b in range(blocks):
        part = slice(b * height, (b + 1) * height)
        position = position + chosen[part] * (before[part] + above[part] + offset)
        last = (b + 1) * height - 1
        filled = above[last : last + 1] + totals[last : last + 1]
        offset = offset + filled + (filled.astype(jnp.int32) & 1).astype(jnp.float32)
    position = position.astype(jnp.int32)
    high = jnp.where(valid, position >> 7, -1)
    low = position & (LANES - 1)

    rows = out.shape[0]
    pieces = [(back & 63).astype(jnp.float32), (back >> 6).astype(jnp.float32), mine.astype(jnp.float32)]
    lane = lax.broadcasted_iota(jnp.int32, (LANES, LANES), 0)
    place = lax.broadcasted_iota(jnp.int32, (rows, LANES), 0)
    found = jnp.zeros((3 * rows, LANES), jnp.float32)
    for r in range(height):
        here = high[r : r + 1] == place
        weights = jnp.concatenate([jnp.where(here, p[r : r + 1], 0.0) for p in pieces], 0)
        spots = (lane == low[r : r + 1]).astype(jnp.float32)
        found = found + lax.dot_general(
            weights.astype(ones), spots.astype(ones), (((1,), (1,)), ((), ())), preferred_element_type=jnp.float32
        )
    words = found.astype(jnp.int32)
    words = words[:rows] + words[rows : 2 * rows] * 64 + words[2 * rows :] * (BASE_MASK + 1)
    end = (place == rows - 1) & (lax.broadcasted_iota(jnp.int32, (rows, LANES), 1) == LANES - 1)
    out[...] = jnp.where(end, (offset * 0.5).astype(jnp.int32), words)


def first_kernel(size, shape, gathered, velocity, x_next, force_out, units, codes, words, sem, *scratch):
    devices, blocks = size
    nrow, ncol, span = shape
    rows = 3 * blocks + LIST_ROWS
    row, col = lax.axis_index("row"), lax.axis_index("col")
    me = row * ncol + col
    holders = [row * ncol + c for c in range(ncol)] + [r * ncol + col for r in range(nrow)]
    codes[...] = jnp.full_like(codes, -1)
    for n, holder in enumerate(holders):
        slot = slot_of(holder, me, devices)
        tile = gathered[pl.ds(pl.multiple_of(slot * rows + 3 * blocks, 8), LIST_ROWS), :]
        codes[pl.ds(n * span, span), :] = tile[:span].astype(jnp.int32)
    build_units(size, shape, codes, words)
    copy = pltpu.make_async_copy(words, units, sem)
    copy.start()
    copy.wait()
    forces = evaluate(size, gathered, rows, units, *scratch)
    for c in range(3):
        at = pl.ds(c * blocks, blocks)
        force_out[at, :] = forces[c]
        x_next[at, :] = gathered[at, :] + TIME_STEP * velocity[at, :] + (0.5 * TIME_STEP * TIME_STEP) * forces[c]


def next_kernel(size, last, gathered, velocity, force, units, x_next, v_next, *rest):
    devices, blocks = size
    if last:
        scratch = rest
    else:
        force_out, *scratch = rest
    forces = evaluate(size, gathered, 3 * blocks, units, *scratch)
    for c in range(3):
        at = pl.ds(c * blocks, blocks)
        x = gathered[at, :]
        v = velocity[at, :] + (0.5 * TIME_STEP) * (force[at, :] + forces[c])
        if last:
            for b in range(blocks):
                lanes = pl.ds(b * LANES, LANES)
                x_next[pl.ds(c, 1), lanes] = x[b : b + 1]
                v_next[pl.ds(c, 1), lanes] = v[b : b + 1]
        else:
            v_next[at, :] = v
            force_out[at, :] = forces[c]
            x_next[at, :] = x + TIME_STEP * v + (0.5 * TIME_STEP * TIME_STEP) * forces[c]


def body(positions, velocities, pair_lists, pair_counts):
    nrow, ncol = lax.axis_size("row"), lax.axis_size("col")
    devices = nrow * ncol
    blocks = positions.shape[1] // LANES
    pairs = pair_lists[0, 0]
    slots = pairs.shape[0]
    size = (devices, blocks)
    span = slots // LANES
    entries = (nrow + ncol) * slots + blocks + 2 * (UNROLL + LEAD)
    unit_rows = 8 * (entries // (8 * LANES) + 1)
    code_rows = 8 * (-(-(nrow + ncol) * span // 8))
    flat = jax.ShapeDtypeStruct((3 * blocks, LANES), jnp.float32)
    whole = jax.ShapeDtypeStruct(positions.shape, jnp.float32)
    unit_list = jax.ShapeDtypeStruct((unit_rows, LANES), jnp.int32)
    vmem = pl.BlockSpec(memory_space=pltpu.VMEM)
    smem = pl.BlockSpec(memory_space=pltpu.SMEM)
    scratch = [
        pltpu.VMEM(((devices + 3) * 4 * blocks, LANES), jnp.float32),
        pltpu.VMEM((blocks, 48, LANES), jnp.bfloat16),
        pltpu.VMEM((blocks * 32, LANES), jnp.float32),
        pltpu.VMEM((LEAD, 2 * LANES, 48), jnp.bfloat16),
        pltpu.VMEM((LEAD, 32, 2 * LANES), jnp.bfloat16),
        pltpu.VMEM((LAG, 2 * LANES, 2 * LANES), jnp.bfloat16),
        pltpu.VMEM((LAG, 32, 2 * LANES), jnp.bfloat16),
    ]
    params = pltpu.CompilerParams(vmem_limit_bytes=48 * 1024 * 1024)

    packed, velocity = pl.pallas_call(
        functools.partial(prepare_kernel, blocks, nrow * blocks),
        out_shape=[jax.ShapeDtypeStruct((3 * blocks + LIST_ROWS, LANES), jnp.float32), flat],
        in_specs=[vmem, vmem, vmem, smem],
        out_specs=[vmem, vmem],
        name="prepare",
    )(positions, velocities, pairs.T, pair_counts)
    gathered = gather(packed, devices)
    current, force, units = pl.pallas_call(
        functools.partial(first_kernel, size, (nrow, ncol, span)),
        out_shape=[flat, flat, unit_list],
        in_specs=[vmem, vmem],
        out_specs=[vmem, vmem, smem],
        scratch_shapes=[
            pltpu.VMEM((code_rows, LANES), jnp.int32),
            pltpu.VMEM((unit_rows, LANES), jnp.int32),
            pltpu.SemaphoreType.DMA,
        ]
        + scratch,
        compiler_params=params,
        name="first_forces",
    )(gathered, velocity)
    for turn in range(STEPS):
        last = turn == STEPS - 1
        result = pl.pallas_call(
            functools.partial(next_kernel, size, last),
            out_shape=[whole] * 2 if last else [flat] * 3,
            in_specs=[vmem, vmem, vmem, smem],
            out_specs=[vmem] * (2 if last else 3),
            scratch_shapes=scratch,
            compiler_params=params,
            name="last_forces" if last else "next_forces",
        )(gather(current, devices), velocity, force, units)
        if last:
            current, velocity = result
        else:
            current, velocity, force = result
    return current, velocity


def solution(mesh):
    placed = (
        P(None, ("row", "col")),
        P(None, ("row", "col")),
        P("row", "col", None, None),
        P("row", "col"),
    )
    return jax.shard_map(
        body,
        mesh=mesh,
        in_specs=placed,
        out_specs=(P(None, ("row", "col")), P(None, ("row", "col"))),
        check_vma=False,
    )
```

```python
import functools

import jax
import jax.numpy as jnp
from jax import lax
from jax.experimental import pallas as pl
from jax.experimental.pallas import tpu as pltpu
from jax.sharding import PartitionSpec as P

ATOM_DEV = 2048
PAIRS_MAX = 256
STEPS = 3
TIME_STEP = 0.5
STIFFNESS = ATOM_DEV / (2048.0 * PAIRS_MAX)

LANES = 128
LIST_ROWS = 8
UNROLL = 32
LEAD = 4
LAG = 8
BASE_BITS = 14
BASE_MASK = (1 << BASE_BITS) - 1
FAR = 1.0e6
AXES = ("row", "col")


def stage_masks(devices):
    bits = devices.bit_length() - 1
    groups = [(0, 1)] if bits else []
    low = 1
    while low < bits:
        high = min(low + 2, bits)
        groups.append((low, high))
        low = high
    return [(lo, 1 << (hi - lo)) for lo, hi in reversed(groups)]


def send(block, devices, mask):
    return lax.ppermute(block, AXES, [(d, d ^ mask(d)) for d in range(devices)])


def send(block, devices, mask):
    return lax.ppermute(block, AXES, [(d, d ^ mask(d)) for d in range(devices)])


def gather_near(block, devices):
    near, far, missing = block, None, [block]
    for number, (low, count) in enumerate(stage_masks(devices)[:-2]):
        if number == 0 and count == 4:
            far = send(block, devices, lambda d: 1)
            both = jnp.concatenate([near, far], 0)
            third = send(near, devices, lambda d: 3 << low)
            whole = send(both, devices, lambda d: (1 + d % 2) << low)
            missing = [whole, third]
            near = jnp.concatenate([near] + missing, 0)
        else:
            parts = [send(near, devices, lambda d: step << low) for step in range(1, count)]
            missing = missing + parts
            near = jnp.concatenate([near] + parts, 0)
    rest = send(jnp.concatenate(missing, 0), devices, lambda d: 1)
    return near, jnp.concatenate([near, rest] if far is None else [near, far, rest], 0)


def gather_last(near, devices, beside=None):
    low, count = stage_masks(devices)[-2]
    parts = [send(near, devices, lambda d: step << low) for step in range(1, count)]
    if beside is not None:
        parts, beside = lax.optimization_barrier((parts, beside))
    parts = jnp.concatenate(parts, 0)
    return parts, send(parts, devices, lambda d: 1), beside


def near_size(devices):
    return devices // 2 // stage_masks(devices)[-2][1]


def slot_of(owner, me, devices):
    relative = owner ^ me
    holder = owner & 1
    place = jnp.zeros_like(relative)
    size = 1
    for number, (low, count) in enumerate(stage_masks(devices)[:-1]):
        step = (relative >> low) & (count - 1)
        if number == 0 and count == 4 and len(stage_masks(devices)) > 2:
            fetcher = jnp.where((step == 1) | (step == 2), step - 1, holder)
            place = jnp.where(step == 0, place, jnp.where(step == 3, 3, 1 + (holder ^ fetcher)))
            holder = fetcher
        else:
            place = place + step * size
        size *= count
    near = near_size(devices)
    other = holder ^ (me & 1)
    return jnp.where(place < near, place + other * near, place + near + other * (size - near))


def prepare_kernel(blocks, span, positions, velocities, pairs, total, out, velocity):
    slots = pairs.shape[1]
    for c in range(3):
        for b in range(blocks):
            at, lanes = pl.ds(c * blocks + b, 1), pl.ds(b * LANES, LANES)
            out[at, :] = positions[pl.ds(c, 1), lanes]
            velocity[at, :] = velocities[pl.ds(c, 1), lanes]
    live = lax.broadcasted_iota(jnp.int32, (1, slots), 1) < total[0, 0]
    code = jnp.where(live, pairs[0:1, :] * span + pairs[1:2, :], -1).astype(jnp.float32)
    out[pl.ds(3 * blocks, LIST_ROWS), :] = jnp.zeros((LIST_ROWS, LANES), jnp.float32)
    for r in range(slots // LANES):
        out[pl.ds(3 * blocks + r, 1), :] = code[:, r * LANES : (r + 1) * LANES]


def matmul(a, b):
    return jnp.dot(a, b, preferred_element_type=jnp.float32)


def split3(tile):
    high = tile.astype(jnp.bfloat16).astype(jnp.float32)
    rest = tile - high
    mid = rest.astype(jnp.bfloat16).astype(jnp.float32)
    return high, mid, rest - mid


def load_points(size, pieces, rows, points):
    devices, blocks = size
    stride = 4 * blocks
    for ref, slots in pieces:
        for n, slot in enumerate(slots):
            norm = None
            for c in range(3):
                y = 0.5 * ref[pl.ds(n * rows + c * blocks, blocks), :]
                points[pl.ds(slot * stride + c * blocks, blocks), :] = y
                norm = y * y if norm is None else norm + y * y
            points[pl.ds(slot * stride + 3 * blocks, blocks), :] = norm
    dummy = devices * stride
    points[pl.ds(dummy, 3 * blocks), :] = jnp.zeros((3 * blocks, LANES), jnp.float32)
    points[pl.ds(dummy + 3 * blocks, blocks), :] = jnp.full((blocks, LANES), FAR, jnp.float32)


def add_pairs(size, part, units, ready, points, lefts, sums, turned_kept, right_kept, weights_kept, partner_kept):
    devices, blocks = size
    stride = 4 * blocks
    dummy = devices * stride
    place = lax.broadcasted_iota(jnp.int32, (8, LANES), 0)
    for b in range(blocks):
        tile = points[pl.ds(b, 8, stride=blocks), :]
        moved = pltpu.roll(tile, 1, 0)
        tile = jnp.where(
            place < 3, 2.0 * tile, jnp.where(place == 3, -1.0, jnp.where(place == 4, 1.0 - moved, 0.0))
        )
        high, mid, low = split3(tile)
        lefts[b] = jnp.concatenate([high, high, high, mid, mid, low], 0).astype(jnp.bfloat16)
    sums[...] = jnp.zeros_like(sums)
    ready()
    steps = [units[units.shape[0] - 1, LANES - 1 - n] for n in range(2)]
    begin, end = {0: (0, steps[0]), 1: (steps[0], steps[1]), None: (0, steps[1])}[part]

    def right_tile(word):
        tile = points[pl.ds(dummy - (word & BASE_MASK), 8, stride=blocks), :]
        tile = jnp.where(place < 4, tile, jnp.where(place == 4, 1.0, 0.0))
        high, mid, low = split3(tile)
        return jnp.concatenate([high, mid, low, high, mid, high], 0).astype(jnp.bfloat16)

    def word(unit, n):
        at = 2 * unit + n
        return units[at >> 7, at & (LANES - 1)]

    def block_of(unit):
        return word(unit, 0) >> BASE_BITS

    def fetch(unit):
        rights = [right_tile(word(unit, n)) for n in range(2)]
        return jnp.concatenate([r.T for r in rights], 0), jnp.concatenate([r[:32] for r in rights], 1)

    def weigh(unit, turned):
        w = jnp.maximum(matmul(turned, lefts[block_of(unit)]), 0.0)
        high = w.astype(jnp.bfloat16)
        return jnp.concatenate([high, (w - high.astype(jnp.float32)).astype(jnp.bfloat16)], 1)

    def add(unit, right, w):
        part = matmul(right, w)
        at = pl.ds(pl.multiple_of(block_of(unit) * 32, 32), 32)
        sums[at, :] = sums[at, :] + (part[:, :LANES] + part[:, LANES:])

    for k in range(LEAD):
        turned_kept[k], right_kept[k] = fetch(begin * UNROLL + k)
    weights_kept[...] = jnp.zeros_like(weights_kept)
    partner_kept[...] = jnp.zeros_like(partner_kept)

    def group(number, carry):
        first = number * UNROLL
        fetched = [(turned_kept[k], right_kept[k]) for k in range(LEAD)]
        weighed = [(partner_kept[k], weights_kept[k]) for k in range(LAG)]
        for k in range(UNROLL):
            add(jnp.maximum(first + k - LAG, 0), *weighed[k])
            turned, right = fetched[k]
            weighed.append((right, weigh(first + k, turned)))
            fetched.append(fetch(first + k + LEAD))
        for k in range(LEAD):
            turned_kept[k], right_kept[k] = fetched[UNROLL + k]
        for k in range(LAG):
            partner_kept[k], weights_kept[k] = weighed[UNROLL + k]
        return carry

    lax.fori_loop(begin, end, group, 0)
    for k in range(LAG):
        add(jnp.maximum(end * UNROLL - LAG + k, 0), partner_kept[k], weights_kept[k])


def forces_of(blocks, points, all_sums):
    def entry(n):
        at = pl.ds(n, blocks, stride=32)
        return sum(sums[at, :] for sums in all_sums)

    total = entry(4)
    forces = []
    for c in range(3):
        y = points[pl.ds(c * blocks, blocks), :]
        forces.append((2.0 * STIFFNESS) * (y * total - (entry(c) + entry(8 + c) + entry(16 + c))))
    return forces


def build_units(size, shape, codes, out):
    devices, blocks = size
    nrow, ncol, span = shape
    row, col = lax.axis_index("row"), lax.axis_index("col")
    me = row * ncol + col
    shift = blocks.bit_length() - 1
    cshift = ncol.bit_length() - 1
    wide = (nrow * blocks).bit_length() - 1
    code = codes[...]
    height = code.shape[0]
    holder = lax.broadcasted_iota(jnp.int32, code.shape, 0) // span
    by_row = holder < ncol
    valid = (code >= 0) & (holder < ncol + nrow)
    left, right = code >> wide, code & (nrow * blocks - 1)
    left_owner = jnp.where(by_row, row, holder - ncol) * ncol + (left >> shift)
    right_owner = ((right >> shift) << cshift) + jnp.where(by_row, holder, col)
    left_place, right_place = left & (blocks - 1), right & (blocks - 1)
    distinct = (left_owner != right_owner) | (left_place != right_place)
    mine = jnp.where(by_row, left_place, right_place)
    owner = jnp.where(by_row, left_owner, right_owner)
    valid = valid & (owner == me) & (by_row | distinct)
    other = jnp.where(by_row, right_owner, left_owner)
    place = jnp.where(by_row, right_place, left_place)
    slot = slot_of(other, me, devices)
    back = (devices - slot) * (4 * blocks) - place
    group = jnp.where(valid, jnp.where(slot < 2 * near_size(devices), mine, mine + blocks), -1)

    ones = jnp.bfloat16
    groups = 2 * blocks
    chosen = jnp.concatenate([(group == g).astype(jnp.float32) for g in range(groups)], 0)
    picked = chosen.astype(ones)
    one, two = lax.broadcasted_iota(jnp.int32, (LANES, LANES), 0), lax.broadcasted_iota(jnp.int32, (LANES, LANES), 1)
    before = matmul(picked, (one < two).astype(jnp.float32).astype(ones))
    totals = matmul(picked, jnp.ones((LANES, LANES), ones))
    lane = lax.broadcasted_iota(jnp.int32, code.shape, 1)
    table = jnp.zeros(code.shape, jnp.float32)
    for g in range(groups):
        table = jnp.where(lane == g, totals[g * height : (g + 1) * height], table)
    row_one, row_two = [lax.broadcasted_iota(jnp.int32, (height, height), n) for n in range(2)]
    above = matmul((row_two < row_one).astype(jnp.float32).astype(ones), table.astype(ones))
    filled = jnp.broadcast_to(above[height - 1 :] + table[height - 1 :], (8, LANES)).astype(jnp.int32)
    filled = filled + (filled & 1)
    pieces = [(filled & 63).astype(jnp.float32).astype(ones), (filled >> 6).astype(jnp.float32).astype(ones)]

    def total_over(mask):
        mask = mask.astype(jnp.float32).astype(ones)
        return matmul(pieces[0], mask) + 64.0 * matmul(pieces[1], mask)

    in_near = one < blocks
    step = 2 * UNROLL
    near_steps = (total_over(in_near).astype(jnp.int32) + step - 1) >> (step.bit_length() - 1)
    far_steps = (total_over(~in_near).astype(jnp.int32) + step - 1) >> (step.bit_length() - 1)
    offset = total_over((one < two) & (in_near == (two < blocks)))
    offset = offset + jnp.where(two[:8] < blocks, 0, near_steps * step).astype(jnp.float32)
    start = above + offset[:1]
    position = jnp.zeros(code.shape, jnp.float32)
    for g in range(groups):
        part = slice(g * height, (g + 1) * height)
        position = position + chosen[part] * (before[part] + start[:, g : g + 1])
    position = position.astype(jnp.int32)
    high = jnp.where(valid, position >> 7, -1)
    low = position & (LANES - 1)

    rows = out.shape[0]
    pieces = [(back & 63).astype(jnp.float32), (back >> 6).astype(jnp.float32), mine.astype(jnp.float32)]
    lane = lax.broadcasted_iota(jnp.int32, (LANES, LANES), 0)
    place = lax.broadcasted_iota(jnp.int32, (rows, LANES), 0)
    found = jnp.zeros((3 * rows, LANES), jnp.float32)
    for r in range(height):
        here = high[r : r + 1] == place
        weights = jnp.concatenate([jnp.where(here, p[r : r + 1], 0.0) for p in pieces], 0)
        spots = (lane == low[r : r + 1]).astype(jnp.float32)
        found = found + lax.dot_general(
            weights.astype(ones), spots.astype(ones), (((1,), (1,)), ((), ())), preferred_element_type=jnp.float32
        )
    words = found.astype(jnp.int32)
    words = words[:rows] + words[rows : 2 * rows] * 64 + words[2 * rows :] * (BASE_MASK + 1)
    lane = lax.broadcasted_iota(jnp.int32, (rows, LANES), 1)
    words = jnp.where((place == rows - 1) & (lane == LANES - 1), near_steps[:1], words)
    out[...] = jnp.where((place == rows - 1) & (lane == LANES - 2), (near_steps + far_steps)[:1], words)


def slot_ranges(devices):
    near = 2 * near_size(devices)
    middle = near + (devices - near) // 2
    return range(near), range(near, middle), range(middle, devices)


def first_kernel(size, shape, near, middle, far, velocity, x_next, force_out, words, codes, units, sem, *scratch):
    devices, blocks = size
    nrow, ncol, span = shape
    rows = 3 * blocks + LIST_ROWS
    row, col = lax.axis_index("row"), lax.axis_index("col")
    me = row * ncol + col
    holders = [row * ncol + c for c in range(ncol)] + [r * ncol + col for r in range(nrow)]
    codes[...] = jnp.full_like(codes, -1)
    pieces = list(zip((near, middle, far), slot_ranges(devices)))
    for n, holder in enumerate(holders):
        slot = slot_of(holder, me, devices)
        for ref, slots in pieces:

            @pl.when((slot >= slots[0]) & (slot <= slots[-1]))
            def _(ref=ref, slots=slots):
                at = pl.multiple_of((slot - slots[0]) * rows + 3 * blocks, 8)
                tile = ref[pl.ds(at, LIST_ROWS), :]
                codes[pl.ds(n * span, span), :] = tile[:span].astype(jnp.int32)

    build_units(size, shape, codes, words)
    copy = pltpu.make_async_copy(words, units, sem)
    copy.start()
    load_points(size, pieces, rows, scratch[0])
    add_pairs(size, None, units, copy.wait, *scratch)
    forces = forces_of(blocks, scratch[0], [scratch[2]])
    for c in range(3):
        at = pl.ds(c * blocks, blocks)
        force_out[at, :] = forces[c]
        x_next[at, :] = near[at, :] + TIME_STEP * velocity[at, :] + (0.5 * TIME_STEP * TIME_STEP) * forces[c]


def near_kernel(size, near, words, sums_out, units, sem, points, lefts, *kept):
    devices, blocks = size
    copy = pltpu.make_async_copy(words, units, sem)
    copy.start()
    load_points(size, [(near, slot_ranges(devices)[0])], 3 * blocks, points)
    add_pairs(size, 0, units, copy.wait, points, lefts, sums_out, *kept)


def next_kernel(size, last, near, middle, far, near_sums, velocity, force, words, x_next, v_next, *rest):
    devices, blocks = size
    if not last:
        force_out, *rest = rest
    units, sem, points, lefts, sums, *kept = rest
    copy = pltpu.make_async_copy(words, units, sem)
    copy.start()
    _, *ranges = slot_ranges(devices)
    load_points(size, [(near, range(1))] + list(zip((middle, far), ranges)), 3 * blocks, points)
    add_pairs(size, 1, units, copy.wait, points, lefts, sums, *kept)
    forces = forces_of(blocks, points, [near_sums, sums])
    for c in range(3):
        at = pl.ds(c * blocks, blocks)
        x = near[at, :]
        v = velocity[at, :] + (0.5 * TIME_STEP) * (force[at, :] + forces[c])
        if last:
            for b in range(blocks):
                lanes = pl.ds(b * LANES, LANES)
                x_next[pl.ds(c, 1), lanes] = x[b : b + 1]
                v_next[pl.ds(c, 1), lanes] = v[b : b + 1]
        else:
            v_next[at, :] = v
            force_out[at, :] = forces[c]
            x_next[at, :] = x + TIME_STEP * v + (0.5 * TIME_STEP * TIME_STEP) * forces[c]


def body(positions, velocities, pair_lists, pair_counts):
    nrow, ncol = lax.axis_size("row"), lax.axis_size("col")
    devices = nrow * ncol
    blocks = positions.shape[1] // LANES
    pairs = pair_lists[0, 0]
    slots = pairs.shape[0]
    size = (devices, blocks)
    span = slots // LANES
    entries = (nrow + ncol) * slots + 2 * blocks + 2 * (2 * UNROLL + LEAD)
    unit_rows = 8 * (entries // (8 * LANES) + 1)
    code_rows = 8 * (-(-(nrow + ncol) * span // 8))
    flat = jax.ShapeDtypeStruct((3 * blocks, LANES), jnp.float32)
    whole = jax.ShapeDtypeStruct(positions.shape, jnp.float32)
    unit_list = jax.ShapeDtypeStruct((unit_rows, LANES), jnp.int32)
    vmem = pl.BlockSpec(memory_space=pltpu.VMEM)
    smem = pl.BlockSpec(memory_space=pltpu.SMEM)
    points = pltpu.VMEM(((devices + 3) * 4 * blocks, LANES), jnp.float32)
    lefts = pltpu.VMEM((blocks, 48, LANES), jnp.bfloat16)
    sums = pltpu.VMEM((blocks * 32, LANES), jnp.float32)
    kept = [
        pltpu.VMEM((LEAD, 2 * LANES, 48), jnp.bfloat16),
        pltpu.VMEM((LEAD, 32, 2 * LANES), jnp.bfloat16),
        pltpu.VMEM((LAG, 2 * LANES, 2 * LANES), jnp.bfloat16),
        pltpu.VMEM((LAG, 32, 2 * LANES), jnp.bfloat16),
    ]
    listed = [pltpu.SMEM((unit_rows, LANES), jnp.int32), pltpu.SemaphoreType.DMA]
    params = pltpu.CompilerParams(vmem_limit_bytes=48 * 1024 * 1024)

    def cost(share):
        flops = int(share * 4e9)
        return pl.CostEstimate(flops=flops, bytes_accessed=1 << 20, transcendentals=0)

    packed, velocity = pl.pallas_call(
        functools.partial(prepare_kernel, blocks, nrow * blocks),
        out_shape=[jax.ShapeDtypeStruct((3 * blocks + LIST_ROWS, LANES), jnp.float32), flat],
        in_specs=[vmem, vmem, vmem, smem],
        out_specs=[vmem, vmem],
        name="prepare",
    )(positions, velocities, pairs.T, pair_counts)
    near, both = gather_near(packed, devices)
    current, force, words = pl.pallas_call(
        functools.partial(first_kernel, size, (nrow, ncol, span)),
        out_shape=[flat, flat, unit_list],
        in_specs=[vmem] * 4,
        out_specs=[vmem] * 3,
        scratch_shapes=[pltpu.VMEM((code_rows, LANES), jnp.int32)] + listed + [points, lefts, sums] + kept,
        compiler_params=params,
        cost_estimate=cost(1.0),
        name="first_forces",
    )(both, *gather_last(near, devices)[:2], velocity)
    for turn in range(STEPS):
        last = turn == STEPS - 1
        near, both = gather_near(current, devices)
        near_sums = pl.pallas_call(
            functools.partial(near_kernel, size),
            out_shape=jax.ShapeDtypeStruct((blocks * 32, LANES), jnp.float32),
            in_specs=[vmem] * 2,
            out_specs=vmem,
            scratch_shapes=listed + [points, lefts] + kept,
            compiler_params=params,
            cost_estimate=cost(0.25),
            name="near_forces",
        )(both, words)
        result = pl.pallas_call(
            functools.partial(next_kernel, size, last),
            out_shape=[whole] * 2 if last else [flat] * 3,
            in_specs=[vmem] * 7,
            out_specs=[vmem] * (2 if last else 3),
            scratch_shapes=listed + [points, lefts, sums] + kept,
            compiler_params=params,
            cost_estimate=cost(0.75),
            name="last_forces" if last else "next_forces",
        )(both, *gather_last(near, devices, near_sums), velocity, force, words)
        if last:
            current, velocity = result
        else:
            current, velocity, force = result
    return current, velocity


def solution(mesh):
    placed = (
        P(None, ("row", "col")),
        P(None, ("row", "col")),
        P("row", "col", None, None),
        P("row", "col"),
    )
    return jax.shard_map(
        body,
        mesh=mesh,
        in_specs=placed,
        out_specs=(P(None, ("row", "col")), P(None, ("row", "col"))),
        check_vma=False,
    )
```

```python
import functools

import jax
import jax.numpy as jnp
from jax import lax
from jax.experimental import pallas as pl
from jax.experimental.pallas import tpu as pltpu
from jax.sharding import PartitionSpec as P

ATOM_DEV = 2048
PAIRS_MAX = 256
STEPS = 3
TIME_STEP = 0.5
STIFFNESS = ATOM_DEV / (2048.0 * PAIRS_MAX)

LANES = 128
LIST_ROWS = 8
STEP = 16
LEAD = 2
LAG = 6
BASE_BITS = 14
BASE_MASK = (1 << BASE_BITS) - 1
FAR = 1.0e6
AXES = ("row", "col")


def stage_masks(devices):
    bits = devices.bit_length() - 1
    groups = [(0, 1)] if bits else []
    low = 1
    while low < bits:
        high = min(low + 2, bits)
        groups.append((low, high))
        low = high
    return [(lo, 1 << (hi - lo)) for lo, hi in reversed(groups)]


def send(block, devices, mask):
    return lax.ppermute(block, AXES, [(d, d ^ mask(d)) for d in range(devices)])


def send(block, devices, mask):
    return lax.ppermute(block, AXES, [(d, d ^ mask(d)) for d in range(devices)])


def gather_near(block, devices):
    near, far, missing = block, None, [block]
    for number, (low, count) in enumerate(stage_masks(devices)[:-2]):
        if number == 0 and count == 4:
            far = send(block, devices, lambda d: 1)
            both = jnp.concatenate([near, far], 0)
            third = send(near, devices, lambda d: 3 << low)
            whole = send(both, devices, lambda d: (1 + d % 2) << low)
            missing = [whole, third]
            near = jnp.concatenate([near] + missing, 0)
        else:
            parts = [send(near, devices, lambda d: step << low) for step in range(1, count)]
            missing = missing + parts
            near = jnp.concatenate([near] + parts, 0)
    rest = send(jnp.concatenate(missing, 0), devices, lambda d: 1)
    return near, jnp.concatenate([near, rest] if far is None else [near, far, rest], 0)


def gather_last(near, devices):
    low, count = stage_masks(devices)[-2]
    return [send(near, devices, lambda d: step << low) for step in range(1, count)]


def exchange(parts, devices):
    parts = jnp.concatenate(parts, 0)
    return parts, send(parts, devices, lambda d: 1)


def near_size(devices):
    return devices // 2 // stage_masks(devices)[-2][1]


def slot_of(owner, me, devices):
    relative = owner ^ me
    holder = owner & 1
    place = jnp.zeros_like(relative)
    size = 1
    for number, (low, count) in enumerate(stage_masks(devices)[:-1]):
        step = (relative >> low) & (count - 1)
        if number == 0 and count == 4 and len(stage_masks(devices)) > 2:
            fetcher = jnp.where((step == 1) | (step == 2), step - 1, holder)
            place = jnp.where(step == 0, place, jnp.where(step == 3, 3, 1 + (holder ^ fetcher)))
            holder = fetcher
        else:
            place = place + step * size
        size *= count
    near = near_size(devices)
    other = holder ^ (me & 1)
    return jnp.where(place < near, place + other * near, place + near + other * (size - near))


def prepare_kernel(blocks, span, positions, velocities, pairs, total, out, velocity):
    slots = pairs.shape[1]
    for c in range(3):
        for b in range(blocks):
            at, lanes = pl.ds(c * blocks + b, 1), pl.ds(b * LANES, LANES)
            out[at, :] = positions[pl.ds(c, 1), lanes]
            velocity[at, :] = velocities[pl.ds(c, 1), lanes]
    live = lax.broadcasted_iota(jnp.int32, (1, slots), 1) < total[0, 0]
    code = jnp.where(live, pairs[0:1, :] * span + pairs[1:2, :], -1).astype(jnp.float32)
    out[pl.ds(3 * blocks, LIST_ROWS), :] = jnp.zeros((LIST_ROWS, LANES), jnp.float32)
    for r in range(slots // LANES):
        out[pl.ds(3 * blocks + r, 1), :] = code[:, r * LANES : (r + 1) * LANES]


def matmul(a, b):
    return jnp.dot(a, b, preferred_element_type=jnp.float32)


def split3(tile):
    high = tile.astype(jnp.bfloat16).astype(jnp.float32)
    rest = tile - high
    mid = rest.astype(jnp.bfloat16).astype(jnp.float32)
    return high, mid, rest - mid


def load_points(size, pieces, rows, points):
    devices, blocks = size
    stride = 4 * blocks
    for ref, first, slots in pieces:
        for n, slot in enumerate(slots, first):
            norm = None
            for c in range(3):
                y = 0.5 * ref[pl.ds(n * rows + c * blocks, blocks), :]
                points[pl.ds(slot * stride + c * blocks, blocks), :] = y
                norm = y * y if norm is None else norm + y * y
            points[pl.ds(slot * stride + 3 * blocks, blocks), :] = norm
    dummy = devices * stride
    points[pl.ds(dummy, 3 * blocks), :] = jnp.zeros((3 * blocks, LANES), jnp.float32)
    points[pl.ds(dummy + 3 * blocks, blocks), :] = jnp.full((blocks, LANES), FAR, jnp.float32)


def add_pairs(size, part, units, ready, points, lefts, sums, turned_kept, right_kept, weights_kept, partner_kept):
    devices, blocks = size
    stride = 4 * blocks
    dummy = devices * stride
    place = lax.broadcasted_iota(jnp.int32, (8, LANES), 0)
    for b in range(blocks):
        tile = points[pl.ds(b, 8, stride=blocks), :]
        moved = pltpu.roll(tile, 1, 0)
        tile = jnp.where(
            place < 3, 2.0 * tile, jnp.where(place == 3, -1.0, jnp.where(place == 4, 1.0 - moved, 0.0))
        )
        high, mid, low = split3(tile)
        lefts[b] = jnp.concatenate([high, high, high, mid, mid, low], 0).astype(jnp.bfloat16)
    sums[...] = jnp.zeros_like(sums)
    ready()
    steps = [units[0, n] for n in range(2)]
    begin, end = {0: (0, steps[0]), 1: (steps[0], steps[1]), None: (0, steps[1])}[part]

    def right_tile(word):
        tile = points[pl.ds(dummy - (word & BASE_MASK), 8, stride=blocks), :]
        tile = jnp.where(place < 4, tile, jnp.where(place == 4, 1.0, 0.0))
        high, mid, low = split3(tile)
        return jnp.concatenate([high, mid, low, high, mid, high], 0).astype(jnp.bfloat16)

    def word(unit, n):
        at = 2 * unit + n + LANES
        return units[at >> 7, at & (LANES - 1)]

    def block_of(unit):
        return word(unit, 0) >> BASE_BITS

    def fetch(unit):
        rights = [right_tile(word(unit, n)) for n in range(2)]
        return jnp.concatenate([r.T for r in rights], 0), jnp.concatenate([r[:32] for r in rights], 1)

    def weigh(unit, turned):
        w = jnp.maximum(matmul(turned, lefts[block_of(unit)]), 0.0)
        high = w.astype(jnp.bfloat16)
        return jnp.concatenate([high, (w - high.astype(jnp.float32)).astype(jnp.bfloat16)], 1)

    def add(unit, right, w):
        part = matmul(right, w)
        at = pl.ds(pl.multiple_of(block_of(unit) * 32, 32), 32)
        sums[at, :] = sums[at, :] + (part[:, :LANES] + part[:, LANES:])

    for k in range(LEAD):
        turned_kept[k], right_kept[k] = fetch(begin * STEP + k)
    weights_kept[...] = jnp.zeros_like(weights_kept)
    partner_kept[...] = jnp.zeros_like(partner_kept)

    def group(first, many):
        fetched = [(turned_kept[k], right_kept[k]) for k in range(LEAD)]
        weighed = [(partner_kept[k], weights_kept[k]) for k in range(LAG)]
        for k in range(many):
            add(jnp.maximum(first + k - LAG, 0), *weighed[k])
            turned, right = fetched[k]
            weighed.append((right, weigh(first + k, turned)))
            fetched.append(fetch(first + k + LEAD))
        for k in range(LEAD):
            turned_kept[k], right_kept[k] = fetched[many + k]
        for k in range(LAG):
            partner_kept[k], weights_kept[k] = weighed[many + k]

    def double(number, carry):
        group((begin + 2 * number) * STEP, 2 * STEP)
        return carry

    lax.fori_loop(0, (end - begin) >> 1, double, 0)

    @pl.when(((end - begin) & 1) == 1)
    def _():
        group((end - 1) * STEP, STEP)

    for k in range(LAG):
        add(jnp.maximum(end * STEP - LAG + k, 0), partner_kept[k], weights_kept[k])


def start_list(words, units, sem):
    copy = pltpu.make_async_copy(words.at[pl.ds(0, 8)], units.at[pl.ds(0, 8)], sem)
    copy.start()

    def ready():
        copy.wait()

        @pl.when(LANES + 2 * (units[0, 1] * STEP + LEAD) > 8 * LANES)
        def _():
            more = pl.ds(8, units.shape[0] - 8)
            rest = pltpu.make_async_copy(words.at[more], units.at[more], sem)
            rest.start()
            rest.wait()

    return ready


def forces_of(blocks, points, all_sums):
    def entry(n):
        at = pl.ds(n, blocks, stride=32)
        return sum(sums[at, :] for sums in all_sums)

    total = entry(4)
    forces = []
    for c in range(3):
        y = points[pl.ds(c * blocks, blocks), :]
        forces.append((2.0 * STIFFNESS) * (y * total - (entry(c) + entry(8 + c) + entry(16 + c))))
    return forces


def build_units(size, shape, codes, out):
    devices, blocks = size
    nrow, ncol, span = shape
    row, col = lax.axis_index("row"), lax.axis_index("col")
    me = row * ncol + col
    shift = blocks.bit_length() - 1
    cshift = ncol.bit_length() - 1
    wide = (nrow * blocks).bit_length() - 1
    code = codes[...]
    height = code.shape[0]
    holder = lax.broadcasted_iota(jnp.int32, code.shape, 0) // span
    by_row = holder < ncol
    valid = (code >= 0) & (holder < ncol + nrow)
    left, right = code >> wide, code & (nrow * blocks - 1)
    left_owner = jnp.where(by_row, row, holder - ncol) * ncol + (left >> shift)
    right_owner = ((right >> shift) << cshift) + jnp.where(by_row, holder, col)
    left_place, right_place = left & (blocks - 1), right & (blocks - 1)
    distinct = (left_owner != right_owner) | (left_place != right_place)
    mine = jnp.where(by_row, left_place, right_place)
    owner = jnp.where(by_row, left_owner, right_owner)
    valid = valid & (owner == me) & (by_row | distinct)
    other = jnp.where(by_row, right_owner, left_owner)
    place = jnp.where(by_row, right_place, left_place)
    slot = slot_of(other, me, devices)
    back = (devices - slot) * (4 * blocks) - place
    group = jnp.where(valid, jnp.where(slot < slot_ranges(devices)[2][0], mine, mine + blocks), -1)

    ones = jnp.bfloat16
    groups = 2 * blocks
    chosen = jnp.concatenate([(group == g).astype(jnp.float32) for g in range(groups)], 0)
    picked = chosen.astype(ones)
    one, two = lax.broadcasted_iota(jnp.int32, (LANES, LANES), 0), lax.broadcasted_iota(jnp.int32, (LANES, LANES), 1)
    before = matmul(picked, (one < two).astype(jnp.float32).astype(ones))
    totals = matmul(picked, jnp.ones((LANES, LANES), ones))
    lane = lax.broadcasted_iota(jnp.int32, code.shape, 1)
    table = jnp.zeros(code.shape, jnp.float32)
    for g in range(groups):
        table = jnp.where(lane == g, totals[g * height : (g + 1) * height], table)
    row_one, row_two = [lax.broadcasted_iota(jnp.int32, (height, height), n) for n in range(2)]
    above = matmul((row_two < row_one).astype(jnp.float32).astype(ones), table.astype(ones))
    filled = jnp.broadcast_to(above[height - 1 :] + table[height - 1 :], (8, LANES)).astype(jnp.int32)
    filled = filled + (filled & 1)
    pieces = [(filled & 63).astype(jnp.float32).astype(ones), (filled >> 6).astype(jnp.float32).astype(ones)]

    def total_over(mask):
        mask = mask.astype(jnp.float32).astype(ones)
        return matmul(pieces[0], mask) + 64.0 * matmul(pieces[1], mask)

    in_near = one < blocks
    step = 2 * STEP
    near_steps = (total_over(in_near).astype(jnp.int32) + step - 1) >> (step.bit_length() - 1)
    far_steps = (total_over(~in_near).astype(jnp.int32) + step - 1) >> (step.bit_length() - 1)
    offset = total_over((one < two) & (in_near == (two < blocks)))
    offset = offset + jnp.where(two[:8] < blocks, 0, near_steps * step).astype(jnp.float32)
    start = above + offset[:1]
    position = jnp.zeros(code.shape, jnp.float32)
    for g in range(groups):
        part = slice(g * height, (g + 1) * height)
        position = position + chosen[part] * (before[part] + start[:, g : g + 1])
    position = position.astype(jnp.int32) + LANES
    high = jnp.where(valid, position >> 7, -1)
    low = position & (LANES - 1)

    rows = out.shape[0]
    pieces = [(back & 63).astype(jnp.float32), (back >> 6).astype(jnp.float32), mine.astype(jnp.float32)]
    lane = lax.broadcasted_iota(jnp.int32, (LANES, LANES), 0)
    place = lax.broadcasted_iota(jnp.int32, (rows, LANES), 0)
    found = jnp.zeros((3 * rows, LANES), jnp.float32)
    for r in range(height):
        here = high[r : r + 1] == place
        weights = jnp.concatenate([jnp.where(here, p[r : r + 1], 0.0) for p in pieces], 0)
        spots = (lane == low[r : r + 1]).astype(jnp.float32)
        found = found + lax.dot_general(
            weights.astype(ones), spots.astype(ones), (((1,), (1,)), ((), ())), preferred_element_type=jnp.float32
        )
    words = found.astype(jnp.int32)
    words = words[:rows] + words[rows : 2 * rows] * 64 + words[2 * rows :] * (BASE_MASK + 1)
    lane = lax.broadcasted_iota(jnp.int32, (rows, LANES), 1)
    words = jnp.where((place == 0) & (lane == 0), near_steps[:1], words)
    out[...] = jnp.where((place == 0) & (lane == 1), (near_steps + far_steps)[:1], words)


def slot_ranges(devices):
    near = near_size(devices)
    middle = near + devices // 2
    return range(2 * near), range(2 * near, 3 * near), range(3 * near, middle), range(middle, devices)


def first_kernel(size, shape, gathered, velocity, x_next, force_out, words, codes, units, sem, *scratch):
    devices, blocks = size
    nrow, ncol, span = shape
    rows = 3 * blocks + LIST_ROWS
    row, col = lax.axis_index("row"), lax.axis_index("col")
    me = row * ncol + col
    holders = [row * ncol + c for c in range(ncol)] + [r * ncol + col for r in range(nrow)]
    codes[...] = jnp.full_like(codes, -1)
    for n, holder in enumerate(holders):
        at = pl.multiple_of(slot_of(holder, me, devices) * rows + 3 * blocks, 8)
        codes[pl.ds(n * span, span), :] = gathered[pl.ds(at, LIST_ROWS), :][:span].astype(jnp.int32)

    build_units(size, shape, codes, words)
    ready = start_list(words, units, sem)
    load_points(size, [(gathered, 0, range(devices))], rows, scratch[0])
    add_pairs(size, None, units, ready, *scratch)
    forces = forces_of(blocks, scratch[0], [scratch[2]])
    for c in range(3):
        at = pl.ds(c * blocks, blocks)
        force_out[at, :] = forces[c]
        x_next[at, :] = gathered[at, :] + TIME_STEP * velocity[at, :] + (0.5 * TIME_STEP * TIME_STEP) * forces[c]


def near_kernel(size, near, part, words, sums_out, units, sem, points, lefts, *kept):
    devices, blocks = size
    ready = start_list(words, units, sem)
    ranges = slot_ranges(devices)
    load_points(size, [(near, 0, ranges[0]), (part, 0, ranges[1])], 3 * blocks, points)
    add_pairs(size, 0, units, ready, points, lefts, sums_out, *kept)


def next_kernel(size, last, near, middle, far, near_sums, velocity, force, words, x_next, v_next, *rest):
    devices, blocks = size
    if not last:
        force_out, *rest = rest
    units, sem, points, lefts, sums, *kept = rest
    ready = start_list(words, units, sem)
    ranges = slot_ranges(devices)
    pieces = [(near, 0, range(1)), (middle, len(ranges[1]), ranges[2]), (far, 0, ranges[3])]
    load_points(size, pieces, 3 * blocks, points)
    add_pairs(size, 1, units, ready, points, lefts, sums, *kept)
    forces = forces_of(blocks, points, [near_sums, sums])
    for c in range(3):
        at = pl.ds(c * blocks, blocks)
        x = near[at, :]
        v = velocity[at, :] + (0.5 * TIME_STEP) * (force[at, :] + forces[c])
        if last:
            for b in range(blocks):
                lanes = pl.ds(b * LANES, LANES)
                x_next[pl.ds(c, 1), lanes] = x[b : b + 1]
                v_next[pl.ds(c, 1), lanes] = v[b : b + 1]
        else:
            v_next[at, :] = v
            force_out[at, :] = forces[c]
            x_next[at, :] = x + TIME_STEP * v + (0.5 * TIME_STEP * TIME_STEP) * forces[c]


def body(positions, velocities, pair_lists, pair_counts):
    nrow, ncol = lax.axis_size("row"), lax.axis_size("col")
    devices = nrow * ncol
    blocks = positions.shape[1] // LANES
    pairs = pair_lists[0, 0]
    slots = pairs.shape[0]
    size = (devices, blocks)
    span = slots // LANES
    entries = LANES + (nrow + ncol) * slots + 2 * blocks + 2 * (3 * STEP + LEAD)
    unit_rows = 8 * (entries // (8 * LANES) + 1)
    code_rows = 8 * (-(-(nrow + ncol) * span // 8))
    flat = jax.ShapeDtypeStruct((3 * blocks, LANES), jnp.float32)
    whole = jax.ShapeDtypeStruct(positions.shape, jnp.float32)
    unit_list = jax.ShapeDtypeStruct((unit_rows, LANES), jnp.int32)
    vmem = pl.BlockSpec(memory_space=pltpu.VMEM)
    smem = pl.BlockSpec(memory_space=pltpu.SMEM)
    points = pltpu.VMEM(((devices + 3) * 4 * blocks, LANES), jnp.float32)
    lefts = pltpu.VMEM((blocks, 48, LANES), jnp.bfloat16)
    sums = pltpu.VMEM((blocks * 32, LANES), jnp.float32)
    kept = [
        pltpu.VMEM((LEAD, 2 * LANES, 48), jnp.bfloat16),
        pltpu.VMEM((LEAD, 32, 2 * LANES), jnp.bfloat16),
        pltpu.VMEM((LAG, 2 * LANES, 2 * LANES), jnp.bfloat16),
        pltpu.VMEM((LAG, 32, 2 * LANES), jnp.bfloat16),
    ]
    listed = [pltpu.SMEM((unit_rows, LANES), jnp.int32), pltpu.SemaphoreType.DMA]
    params = pltpu.CompilerParams(vmem_limit_bytes=48 * 1024 * 1024)

    def cost(share):
        flops = int(share * 4e9)
        return pl.CostEstimate(flops=flops, bytes_accessed=1 << 20, transcendentals=0)

    packed, velocity = pl.pallas_call(
        functools.partial(prepare_kernel, blocks, nrow * blocks),
        out_shape=[jax.ShapeDtypeStruct((3 * blocks + LIST_ROWS, LANES), jnp.float32), flat],
        in_specs=[vmem, vmem, vmem, smem],
        out_specs=[vmem, vmem],
        name="prepare",
    )(positions, velocities, pairs.T, pair_counts)
    near, both = gather_near(packed, devices)
    current, force, words = pl.pallas_call(
        functools.partial(first_kernel, size, (nrow, ncol, span)),
        out_shape=[flat, flat, unit_list],
        in_specs=[vmem] * 2,
        out_specs=[vmem] * 3,
        scratch_shapes=[pltpu.VMEM((code_rows, LANES), jnp.int32)] + listed + [points, lefts, sums] + kept,
        compiler_params=params,
        cost_estimate=cost(1.0),
        name="first_forces",
    )(jnp.concatenate([both, *exchange(gather_last(near, devices), devices)], 0), velocity)
    for turn in range(STEPS):
        last = turn == STEPS - 1
        near, both = gather_near(current, devices)
        parts = gather_last(near, devices)
        near_sums = pl.pallas_call(
            functools.partial(near_kernel, size),
            out_shape=jax.ShapeDtypeStruct((blocks * 32, LANES), jnp.float32),
            in_specs=[vmem] * 3,
            out_specs=vmem,
            scratch_shapes=listed + [points, lefts] + kept,
            compiler_params=params,
            cost_estimate=cost(0.25),
            name="near_forces",
        )(both, parts[0], words)
        parts, near_sums = lax.optimization_barrier((parts, near_sums))
        result = pl.pallas_call(
            functools.partial(next_kernel, size, last),
            out_shape=[whole] * 2 if last else [flat] * 3,
            in_specs=[vmem] * 7,
            out_specs=[vmem] * (2 if last else 3),
            scratch_shapes=listed + [points, lefts, sums] + kept,
            compiler_params=params,
            cost_estimate=cost(0.75),
            name="last_forces" if last else "next_forces",
        )(both, *exchange(parts, devices), near_sums, velocity, force, words)
        if last:
            current, velocity = result
        else:
            current, velocity, force = result
    return current, velocity


def solution(mesh):
    placed = (
        P(None, ("row", "col")),
        P(None, ("row", "col")),
        P("row", "col", None, None),
        P("row", "col"),
    )
    return jax.shard_map(
        body,
        mesh=mesh,
        in_specs=placed,
        out_specs=(P(None, ("row", "col")), P(None, ("row", "col"))),
        check_vma=False,
    )
```

```python
import functools

import jax
import jax.numpy as jnp
from jax import lax
from jax.experimental import pallas as pl
from jax.experimental.pallas import tpu as pltpu
from jax.sharding import PartitionSpec as P

ATOM_DEV = 2048
PAIRS_MAX = 256
STEPS = 3
TIME_STEP = 0.5
STIFFNESS = ATOM_DEV / (2048.0 * PAIRS_MAX)

LANES = 128
LIST_ROWS = 8
SUM_ROWS = 16
STEP = 16
LEAD = 2
LAG = 6
BASE_BITS = 14
BASE_MASK = (1 << BASE_BITS) - 1
FAR = 1.0e6
AXES = ("row", "col")


def stage_masks(devices):
    bits = devices.bit_length() - 1
    groups = [(0, 1)] if bits else []
    low = 1
    while low < bits:
        high = min(low + 2, bits)
        groups.append((low, high))
        low = high
    return [(lo, 1 << (hi - lo)) for lo, hi in reversed(groups)]


def send(block, devices, mask):
    return lax.ppermute(block, AXES, [(d, d ^ mask(d)) for d in range(devices)])


def send(block, devices, mask):
    return lax.ppermute(block, AXES, [(d, d ^ mask(d)) for d in range(devices)])


def gather_near(block, devices):
    near, far, missing = block, None, [block]
    for number, (low, count) in enumerate(stage_masks(devices)[:-2]):
        if number == 0 and count == 4:
            far = send(block, devices, lambda d: 1)
            both = jnp.concatenate([near, far], 0)
            third = send(near, devices, lambda d: 3 << low)
            whole = send(both, devices, lambda d: (1 + d % 2) << low)
            missing = [whole, third]
            near = jnp.concatenate([near] + missing, 0)
        else:
            parts = [send(near, devices, lambda d: step << low) for step in range(1, count)]
            missing = missing + parts
            near = jnp.concatenate([near] + parts, 0)
    rest = send(jnp.concatenate(missing, 0), devices, lambda d: 1)
    return near, jnp.concatenate([near, rest] if far is None else [near, far, rest], 0)


def gather_last(near, devices):
    low, count = stage_masks(devices)[-2]
    return [send(near, devices, lambda d: step << low) for step in range(1, count)]


def exchange(parts, devices):
    parts = jnp.concatenate(parts, 0)
    return parts, send(parts, devices, lambda d: 1)


def near_size(devices):
    return devices // 2 // stage_masks(devices)[-2][1]


def slot_of(owner, me, devices):
    relative = owner ^ me
    holder = owner & 1
    place = jnp.zeros_like(relative)
    size = 1
    for number, (low, count) in enumerate(stage_masks(devices)[:-1]):
        step = (relative >> low) & (count - 1)
        if number == 0 and count == 4 and len(stage_masks(devices)) > 2:
            fetcher = jnp.where((step == 1) | (step == 2), step - 1, holder)
            place = jnp.where(step == 0, place, jnp.where(step == 3, 3, 1 + (holder ^ fetcher)))
            holder = fetcher
        else:
            place = place + step * size
        size *= count
    near = near_size(devices)
    other = holder ^ (me & 1)
    return jnp.where(place < near, place + other * near, place + near + other * (size - near))


def prepare_kernel(blocks, span, positions, velocities, pairs, total, out, velocity):
    slots = pairs.shape[1]
    for c in range(3):
        for b in range(blocks):
            at, lanes = pl.ds(c * blocks + b, 1), pl.ds(b * LANES, LANES)
            out[at, :] = positions[pl.ds(c, 1), lanes]
            velocity[at, :] = velocities[pl.ds(c, 1), lanes]
    live = lax.broadcasted_iota(jnp.int32, (1, slots), 1) < total[0, 0]
    code = jnp.where(live, pairs[0:1, :] * span + pairs[1:2, :], -1).astype(jnp.float32)
    out[pl.ds(3 * blocks, LIST_ROWS), :] = jnp.zeros((LIST_ROWS, LANES), jnp.float32)
    for r in range(slots // LANES):
        out[pl.ds(3 * blocks + r, 1), :] = code[:, r * LANES : (r + 1) * LANES]


def matmul(a, b):
    return jnp.dot(a, b, preferred_element_type=jnp.float32)


def split3(tile):
    high = tile.astype(jnp.bfloat16).astype(jnp.float32)
    rest = tile - high
    mid = rest.astype(jnp.bfloat16).astype(jnp.float32)
    return high, mid, rest - mid


def load_points(size, pieces, rows, points):
    devices, blocks = size
    stride = 4 * blocks
    for ref, first, slots in pieces:
        for n, slot in enumerate(slots, first):
            norm = None
            for c in range(3):
                y = 0.5 * ref[pl.ds(n * rows + c * blocks, blocks), :]
                points[pl.ds(slot * stride + c * blocks, blocks), :] = y
                norm = y * y if norm is None else norm + y * y
            points[pl.ds(slot * stride + 3 * blocks, blocks), :] = norm
    dummy = devices * stride
    points[pl.ds(dummy, 3 * blocks), :] = jnp.zeros((3 * blocks, LANES), jnp.float32)
    points[pl.ds(dummy + 3 * blocks, blocks), :] = jnp.full((blocks, LANES), FAR, jnp.float32)


def add_pairs(size, part, units, ready, points, lefts, sums, turned_kept, right_kept, weights_kept, partner_kept):
    devices, blocks = size
    stride = 4 * blocks
    dummy = devices * stride
    place = lax.broadcasted_iota(jnp.int32, (8, LANES), 0)
    for b in range(blocks):
        tile = points[pl.ds(b, 8, stride=blocks), :]
        moved = pltpu.roll(tile, 1, 0)
        tile = jnp.where(
            place < 3, 2.0 * tile, jnp.where(place == 3, -1.0, jnp.where(place == 4, 1.0 - moved, 0.0))
        )
        high, mid, low = split3(tile)
        lefts[b] = jnp.concatenate([high, high, high, mid, mid, low], 0).astype(jnp.bfloat16)
    sums[...] = jnp.zeros_like(sums)
    ready()
    steps = [units[0, n] for n in range(2)]
    begin, end = {0: (0, steps[0]), 1: (steps[0], steps[1]), None: (0, steps[1])}[part]

    def right_tile(word):
        tile = points[pl.ds(dummy - (word & BASE_MASK), 8, stride=blocks), :]
        tile = jnp.where(place < 4, tile, jnp.where(place == 4, 1.0, 0.0))
        high, mid, low = split3(tile)
        stack = jnp.concatenate([high, mid, low, high, mid, high], 0).astype(jnp.bfloat16)
        return stack, jnp.concatenate([high, mid + pltpu.roll(low, 4, 0)], 0).astype(jnp.bfloat16)

    def word(unit, n):
        at = 2 * unit + n + LANES
        return units[at >> 7, at & (LANES - 1)]

    def block_of(unit):
        return word(unit, 0) >> BASE_BITS

    def fetch(unit):
        rights = [right_tile(word(unit, n)) for n in range(2)]
        return jnp.concatenate([r.T for r, _ in rights], 0), jnp.concatenate([r for _, r in rights], 1)

    def weigh(unit, turned):
        w = jnp.maximum(matmul(turned, lefts[block_of(unit)]), 0.0)
        high = w.astype(jnp.bfloat16)
        return jnp.concatenate([high, (w - high.astype(jnp.float32)).astype(jnp.bfloat16)], 1)

    def add(unit, right, w):
        part = matmul(right, w)
        at = pl.ds(pl.multiple_of(block_of(unit) * SUM_ROWS, SUM_ROWS), SUM_ROWS)
        sums[at, :] = sums[at, :] + (part[:, :LANES] + part[:, LANES:])

    for k in range(LEAD):
        turned_kept[k], right_kept[k] = fetch(begin * STEP + k)
    weights_kept[...] = jnp.zeros_like(weights_kept)
    partner_kept[...] = jnp.zeros_like(partner_kept)

    def group(first, many):
        fetched = [(turned_kept[k], right_kept[k]) for k in range(LEAD)]
        weighed = [(partner_kept[k], weights_kept[k]) for k in range(LAG)]
        for k in range(many):
            add(jnp.maximum(first + k - LAG, 0), *weighed[k])
            turned, right = fetched[k]
            weighed.append((right, weigh(first + k, turned)))
            fetched.append(fetch(first + k + LEAD))
        for k in range(LEAD):
            turned_kept[k], right_kept[k] = fetched[many + k]
        for k in range(LAG):
            partner_kept[k], weights_kept[k] = weighed[many + k]

    def double(number, carry):
        group((begin + 2 * number) * STEP, 2 * STEP)
        return carry

    lax.fori_loop(0, (end - begin) >> 1, double, 0)

    @pl.when(((end - begin) & 1) == 1)
    def _():
        group((end - 1) * STEP, STEP)

    for k in range(LAG):
        add(jnp.maximum(end * STEP - LAG + k, 0), partner_kept[k], weights_kept[k])


def start_list(words, units, sem):
    copy = pltpu.make_async_copy(words.at[pl.ds(0, 8)], units.at[pl.ds(0, 8)], sem)
    copy.start()

    def ready():
        copy.wait()

        @pl.when(LANES + 2 * (units[0, 1] * STEP + LEAD) > 8 * LANES)
        def _():
            more = pl.ds(8, units.shape[0] - 8)
            rest = pltpu.make_async_copy(words.at[more], units.at[more], sem)
            rest.start()
            rest.wait()

    return ready


def forces_of(blocks, points, all_sums):
    def entry(n):
        at = pl.ds(n, blocks, stride=SUM_ROWS)
        return sum(sums[at, :] for sums in all_sums)

    total = entry(4)
    forces = []
    for c in range(3):
        y = points[pl.ds(c * blocks, blocks), :]
        forces.append((2.0 * STIFFNESS) * (y * total - (entry(c) + entry(8 + c) + entry(12 + c))))
    return forces


def build_units(size, shape, codes, out):
    devices, blocks = size
    nrow, ncol, span = shape
    row, col = lax.axis_index("row"), lax.axis_index("col")
    me = row * ncol + col
    shift = blocks.bit_length() - 1
    cshift = ncol.bit_length() - 1
    wide = (nrow * blocks).bit_length() - 1
    code = codes[...]
    height = code.shape[0]
    holder = lax.broadcasted_iota(jnp.int32, code.shape, 0) // span
    by_row = holder < ncol
    valid = (code >= 0) & (holder < ncol + nrow)
    left, right = code >> wide, code & (nrow * blocks - 1)
    left_owner = jnp.where(by_row, row, holder - ncol) * ncol + (left >> shift)
    right_owner = ((right >> shift) << cshift) + jnp.where(by_row, holder, col)
    left_place, right_place = left & (blocks - 1), right & (blocks - 1)
    distinct = (left_owner != right_owner) | (left_place != right_place)
    mine = jnp.where(by_row, left_place, right_place)
    owner = jnp.where(by_row, left_owner, right_owner)
    valid = valid & (owner == me) & (by_row | distinct)
    other = jnp.where(by_row, right_owner, left_owner)
    place = jnp.where(by_row, right_place, left_place)
    slot = slot_of(other, me, devices)
    back = (devices - slot) * (4 * blocks) - place
    group = jnp.where(valid, jnp.where(slot < slot_ranges(devices)[2][0], mine, mine + blocks), -1)

    ones = jnp.bfloat16
    groups = 2 * blocks
    chosen = jnp.concatenate([(group == g).astype(jnp.float32) for g in range(groups)], 0)
    picked = chosen.astype(ones)
    one, two = lax.broadcasted_iota(jnp.int32, (LANES, LANES), 0), lax.broadcasted_iota(jnp.int32, (LANES, LANES), 1)
    before = matmul(picked, (one < two).astype(jnp.float32).astype(ones))
    totals = matmul(picked, jnp.ones((LANES, LANES), ones))
    lane = lax.broadcasted_iota(jnp.int32, code.shape, 1)
    table = jnp.zeros(code.shape, jnp.float32)
    for g in range(groups):
        table = jnp.where(lane == g, totals[g * height : (g + 1) * height], table)
    row_one, row_two = [lax.broadcasted_iota(jnp.int32, (height, height), n) for n in range(2)]
    above = matmul((row_two < row_one).astype(jnp.float32).astype(ones), table.astype(ones))
    filled = jnp.broadcast_to(above[height - 1 :] + table[height - 1 :], (8, LANES)).astype(jnp.int32)
    filled = filled + (filled & 1)
    pieces = [(filled & 63).astype(jnp.float32).astype(ones), (filled >> 6).astype(jnp.float32).astype(ones)]

    def total_over(mask):
        mask = mask.astype(jnp.float32).astype(ones)
        return matmul(pieces[0], mask) + 64.0 * matmul(pieces[1], mask)

    in_near = one < blocks
    step = 2 * STEP
    near_steps = (total_over(in_near).astype(jnp.int32) + step - 1) >> (step.bit_length() - 1)
    far_steps = (total_over(~in_near).astype(jnp.int32) + step - 1) >> (step.bit_length() - 1)
    offset = total_over((one < two) & (in_near == (two < blocks)))
    offset = offset + jnp.where(two[:8] < blocks, 0, near_steps * step).astype(jnp.float32)
    start = above + offset[:1]
    position = jnp.zeros(code.shape, jnp.float32)
    for g in range(groups):
        part = slice(g * height, (g + 1) * height)
        position = position + chosen[part] * (before[part] + start[:, g : g + 1])
    position = position.astype(jnp.int32) + LANES
    high = jnp.where(valid, position >> 7, -1)
    low = position & (LANES - 1)

    rows = out.shape[0]
    pieces = [(back & 63).astype(jnp.float32), (back >> 6).astype(jnp.float32), mine.astype(jnp.float32)]
    lane = lax.broadcasted_iota(jnp.int32, (LANES, LANES), 0)
    place = lax.broadcasted_iota(jnp.int32, (rows, LANES), 0)
    found = jnp.zeros((3 * rows, LANES), jnp.float32)
    for r in range(height):
        here = high[r : r + 1] == place
        weights = jnp.concatenate([jnp.where(here, p[r : r + 1], 0.0) for p in pieces], 0)
        spots = (lane == low[r : r + 1]).astype(jnp.float32)
        found = found + lax.dot_general(
            weights.astype(ones), spots.astype(ones), (((1,), (1,)), ((), ())), preferred_element_type=jnp.float32
        )
    words = found.astype(jnp.int32)
    words = words[:rows] + words[rows : 2 * rows] * 64 + words[2 * rows :] * (BASE_MASK + 1)
    lane = lax.broadcasted_iota(jnp.int32, (rows, LANES), 1)
    words = jnp.where((place == 0) & (lane == 0), near_steps[:1], words)
    out[...] = jnp.where((place == 0) & (lane == 1), (near_steps + far_steps)[:1], words)


def slot_ranges(devices):
    near = near_size(devices)
    middle = near + devices // 2
    return range(2 * near), range(2 * near, 3 * near), range(3 * near, middle), range(middle, devices)


def first_kernel(size, shape, gathered, velocity, x_next, force_out, words, codes, units, sem, *scratch):
    devices, blocks = size
    nrow, ncol, span = shape
    rows = 3 * blocks + LIST_ROWS
    row, col = lax.axis_index("row"), lax.axis_index("col")
    me = row * ncol + col
    holders = [row * ncol + c for c in range(ncol)] + [r * ncol + col for r in range(nrow)]
    codes[...] = jnp.full_like(codes, -1)
    for n, holder in enumerate(holders):
        at = pl.multiple_of(slot_of(holder, me, devices) * rows + 3 * blocks, 8)
        codes[pl.ds(n * span, span), :] = gathered[pl.ds(at, LIST_ROWS), :][:span].astype(jnp.int32)

    build_units(size, shape, codes, words)
    ready = start_list(words, units, sem)
    load_points(size, [(gathered, 0, range(devices))], rows, scratch[0])
    add_pairs(size, None, units, ready, *scratch)
    forces = forces_of(blocks, scratch[0], [scratch[2]])
    for c in range(3):
        at = pl.ds(c * blocks, blocks)
        force_out[at, :] = forces[c]
        x_next[at, :] = gathered[at, :] + TIME_STEP * velocity[at, :] + (0.5 * TIME_STEP * TIME_STEP) * forces[c]


def near_kernel(size, near, part, words, sums_out, units, sem, points, lefts, *kept):
    devices, blocks = size
    ready = start_list(words, units, sem)
    ranges = slot_ranges(devices)
    load_points(size, [(near, 0, ranges[0]), (part, 0, ranges[1])], 3 * blocks, points)
    add_pairs(size, 0, units, ready, points, lefts, sums_out, *kept)


def next_kernel(size, last, near, middle, far, near_sums, velocity, force, words, x_next, v_next, *rest):
    devices, blocks = size
    if not last:
        force_out, *rest = rest
    units, sem, points, lefts, sums, *kept = rest
    ready = start_list(words, units, sem)
    ranges = slot_ranges(devices)
    pieces = [(near, 0, range(1)), (middle, len(ranges[1]), ranges[2]), (far, 0, ranges[3])]
    load_points(size, pieces, 3 * blocks, points)
    add_pairs(size, 1, units, ready, points, lefts, sums, *kept)
    forces = forces_of(blocks, points, [near_sums, sums])
    for c in range(3):
        at = pl.ds(c * blocks, blocks)
        x = near[at, :]
        v = velocity[at, :] + (0.5 * TIME_STEP) * (force[at, :] + forces[c])
        if last:
            for b in range(blocks):
                lanes = pl.ds(b * LANES, LANES)
                x_next[pl.ds(c, 1), lanes] = x[b : b + 1]
                v_next[pl.ds(c, 1), lanes] = v[b : b + 1]
        else:
            v_next[at, :] = v
            force_out[at, :] = forces[c]
            x_next[at, :] = x + TIME_STEP * v + (0.5 * TIME_STEP * TIME_STEP) * forces[c]


def body(positions, velocities, pair_lists, pair_counts):
    nrow, ncol = lax.axis_size("row"), lax.axis_size("col")
    devices = nrow * ncol
    blocks = positions.shape[1] // LANES
    pairs = pair_lists[0, 0]
    slots = pairs.shape[0]
    size = (devices, blocks)
    span = slots // LANES
    entries = LANES + (nrow + ncol) * slots + 2 * blocks + 2 * (3 * STEP + LEAD)
    unit_rows = 8 * (entries // (8 * LANES) + 1)
    code_rows = 8 * (-(-(nrow + ncol) * span // 8))
    flat = jax.ShapeDtypeStruct((3 * blocks, LANES), jnp.float32)
    whole = jax.ShapeDtypeStruct(positions.shape, jnp.float32)
    unit_list = jax.ShapeDtypeStruct((unit_rows, LANES), jnp.int32)
    vmem = pl.BlockSpec(memory_space=pltpu.VMEM)
    smem = pl.BlockSpec(memory_space=pltpu.SMEM)
    points = pltpu.VMEM(((devices + 3) * 4 * blocks, LANES), jnp.float32)
    lefts = pltpu.VMEM((blocks, 48, LANES), jnp.bfloat16)
    sums = pltpu.VMEM((blocks * SUM_ROWS, LANES), jnp.float32)
    kept = [
        pltpu.VMEM((LEAD, 2 * LANES, 48), jnp.bfloat16),
        pltpu.VMEM((LEAD, SUM_ROWS, 2 * LANES), jnp.bfloat16),
        pltpu.VMEM((LAG, 2 * LANES, 2 * LANES), jnp.bfloat16),
        pltpu.VMEM((LAG, SUM_ROWS, 2 * LANES), jnp.bfloat16),
    ]
    listed = [pltpu.SMEM((unit_rows, LANES), jnp.int32), pltpu.SemaphoreType.DMA]
    params = pltpu.CompilerParams(vmem_limit_bytes=48 * 1024 * 1024)

    def cost(share):
        flops = int(share * 4e9)
        return pl.CostEstimate(flops=flops, bytes_accessed=1 << 20, transcendentals=0)

    packed, velocity = pl.pallas_call(
        functools.partial(prepare_kernel, blocks, nrow * blocks),
        out_shape=[jax.ShapeDtypeStruct((3 * blocks + LIST_ROWS, LANES), jnp.float32), flat],
        in_specs=[vmem, vmem, vmem, smem],
        out_specs=[vmem, vmem],
        name="prepare",
    )(positions, velocities, pairs.T, pair_counts)
    near, both = gather_near(packed, devices)
    current, force, words = pl.pallas_call(
        functools.partial(first_kernel, size, (nrow, ncol, span)),
        out_shape=[flat, flat, unit_list],
        in_specs=[vmem] * 2,
        out_specs=[vmem] * 3,
        scratch_shapes=[pltpu.VMEM((code_rows, LANES), jnp.int32)] + listed + [points, lefts, sums] + kept,
        compiler_params=params,
        cost_estimate=cost(1.0),
        name="first_forces",
    )(jnp.concatenate([both, *exchange(gather_last(near, devices), devices)], 0), velocity)
    for turn in range(STEPS):
        last = turn == STEPS - 1
        near, both = gather_near(current, devices)
        parts = gather_last(near, devices)
        near_sums = pl.pallas_call(
            functools.partial(near_kernel, size),
            out_shape=jax.ShapeDtypeStruct((blocks * SUM_ROWS, LANES), jnp.float32),
            in_specs=[vmem] * 3,
            out_specs=vmem,
            scratch_shapes=listed + [points, lefts] + kept,
            compiler_params=params,
            cost_estimate=cost(0.25),
            name="near_forces",
        )(both, parts[0], words)
        parts, near_sums = lax.optimization_barrier((parts, near_sums))
        result = pl.pallas_call(
            functools.partial(next_kernel, size, last),
            out_shape=[whole] * 2 if last else [flat] * 3,
            in_specs=[vmem] * 7,
            out_specs=[vmem] * (2 if last else 3),
            scratch_shapes=listed + [points, lefts, sums] + kept,
            compiler_params=params,
            cost_estimate=cost(0.75),
            name="last_forces" if last else "next_forces",
        )(both, *exchange(parts, devices), near_sums, velocity, force, words)
        if last:
            current, velocity = result
        else:
            current, velocity, force = result
    return current, velocity


def solution(mesh):
    placed = (
        P(None, ("row", "col")),
        P(None, ("row", "col")),
        P("row", "col", None, None),
        P("row", "col"),
    )
    return jax.shard_map(
        body,
        mesh=mesh,
        in_specs=placed,
        out_specs=(P(None, ("row", "col")), P(None, ("row", "col"))),
        check_vma=False,
    )
```

```python
import functools

import jax
import jax.numpy as jnp
from jax import lax
from jax.experimental import pallas as pl
from jax.experimental.pallas import tpu as pltpu
from jax.sharding import PartitionSpec as P

ATOM_DEV = 2048
PAIRS_MAX = 256
STEPS = 3
TIME_STEP = 0.5
STIFFNESS = ATOM_DEV / (2048.0 * PAIRS_MAX)

LANES = 128
LIST_ROWS = 8
SUM_ROWS = 16
STEP = 16
LEAD = 2
LAG = 6
BASE_BITS = 14
BASE_MASK = (1 << BASE_BITS) - 1
FAR = 1.0e6
AXES = ("row", "col")


def stage_masks(devices):
    bits = devices.bit_length() - 1
    groups = [(0, 1)] if bits else []
    low = 1
    while low < bits:
        high = min(low + 2, bits)
        groups.append((low, high))
        low = high
    return [(lo, 1 << (hi - lo)) for lo, hi in reversed(groups)]


def send(block, devices, mask):
    return lax.ppermute(block, AXES, [(d, d ^ mask(d)) for d in range(devices)])


def send(block, devices, mask):
    return lax.ppermute(block, AXES, [(d, d ^ mask(d)) for d in range(devices)])


def gather_near(block, devices):
    near, far, missing = block, None, [block]
    for number, (low, count) in enumerate(stage_masks(devices)[:-2]):
        if number == 0 and count == 4:
            far = send(block, devices, lambda d: 1)
            both = jnp.concatenate([near, far], 0)
            third = send(near, devices, lambda d: 3 << low)
            whole = send(both, devices, lambda d: (1 + d % 2) << low)
            missing = [whole, third]
            near = jnp.concatenate([near] + missing, 0)
        else:
            parts = [send(near, devices, lambda d: step << low) for step in range(1, count)]
            missing = missing + parts
            near = jnp.concatenate([near] + parts, 0)
    rest = send(jnp.concatenate(missing, 0), devices, lambda d: 1)
    return near, jnp.concatenate([near, rest] if far is None else [near, far, rest], 0)


def gather_last(near, devices):
    low, count = stage_masks(devices)[-2]
    return [send(near, devices, lambda d: step << low) for step in range(1, count)]


def exchange(parts, devices):
    parts = jnp.concatenate(parts, 0)
    return parts, send(parts, devices, lambda d: 1)


def near_size(devices):
    return devices // 2 // stage_masks(devices)[-2][1]


def slot_of(owner, me, devices):
    relative = owner ^ me
    holder = owner & 1
    place = jnp.zeros_like(relative)
    size = 1
    for number, (low, count) in enumerate(stage_masks(devices)[:-1]):
        step = (relative >> low) & (count - 1)
        if number == 0 and count == 4 and len(stage_masks(devices)) > 2:
            fetcher = jnp.where((step == 1) | (step == 2), step - 1, holder)
            place = jnp.where(step == 0, place, jnp.where(step == 3, 3, 1 + (holder ^ fetcher)))
            holder = fetcher
        else:
            place = place + step * size
        size *= count
    near = near_size(devices)
    other = holder ^ (me & 1)
    return jnp.where(place < near, place + other * near, place + near + other * (size - near))


def prepare_kernel(blocks, span, positions, velocities, pairs, total, out, velocity):
    slots = pairs.shape[1]
    for c in range(3):
        for b in range(blocks):
            at, lanes = pl.ds(c * blocks + b, 1), pl.ds(b * LANES, LANES)
            out[at, :] = positions[pl.ds(c, 1), lanes]
            velocity[at, :] = velocities[pl.ds(c, 1), lanes]
    live = lax.broadcasted_iota(jnp.int32, (1, slots), 1) < total[0, 0]
    code = jnp.where(live, pairs[0:1, :] * span + pairs[1:2, :], -1).astype(jnp.float32)
    out[pl.ds(3 * blocks, LIST_ROWS), :] = jnp.zeros((LIST_ROWS, LANES), jnp.float32)
    for r in range(slots // LANES):
        out[pl.ds(3 * blocks + r, 1), :] = code[:, r * LANES : (r + 1) * LANES]


def matmul(a, b):
    return jnp.dot(a, b, preferred_element_type=jnp.float32)


def split3(tile):
    high = tile.astype(jnp.bfloat16).astype(jnp.float32)
    rest = tile - high
    mid = rest.astype(jnp.bfloat16).astype(jnp.float32)
    return high, mid, rest - mid


def load_points(size, pieces, rows, points):
    devices, blocks = size
    stride = 4 * blocks
    for ref, first, slots in pieces:
        for n, slot in enumerate(slots, first):
            norm = None
            for c in range(3):
                y = 0.5 * ref[pl.ds(n * rows + c * blocks, blocks), :]
                points[pl.ds(slot * stride + c * blocks, blocks), :] = y
                norm = y * y if norm is None else norm + y * y
            points[pl.ds(slot * stride + 3 * blocks, blocks), :] = norm
    dummy = devices * stride
    points[pl.ds(dummy, 3 * blocks), :] = jnp.zeros((3 * blocks, LANES), jnp.float32)
    points[pl.ds(dummy + 3 * blocks, blocks), :] = jnp.full((blocks, LANES), FAR, jnp.float32)


def add_pairs(size, part, units, ready, points, lefts, sums, turned_kept, right_kept, weights_kept, partner_kept):
    devices, blocks = size
    stride = 4 * blocks
    dummy = devices * stride
    place = lax.broadcasted_iota(jnp.int32, (8, LANES), 0)
    for b in range(blocks):
        tile = points[pl.ds(b, 8, stride=blocks), :]
        moved = pltpu.roll(tile, 1, 0)
        tile = jnp.where(
            place < 3, 2.0 * tile, jnp.where(place == 3, -1.0, jnp.where(place == 4, 1.0 - moved, 0.0))
        )
        high, mid, low = split3(tile)
        lefts[b] = jnp.concatenate([high, high, high, mid, mid, low], 0).astype(jnp.bfloat16)
    sums[...] = jnp.zeros_like(sums)
    ready()
    steps = [units[0, n] for n in range(2)]
    begin, end = {0: (0, steps[0]), 1: (steps[0], steps[1]), None: (0, steps[1])}[part]

    def right_tile(word):
        tile = points[pl.ds(dummy - (word & BASE_MASK), 8, stride=blocks), :]
        tile = jnp.where(place < 4, tile, jnp.where(place == 4, 1.0, 0.0))
        high, mid, low = split3(tile)
        stack = jnp.concatenate([high, mid, low, high, mid, high], 0).astype(jnp.bfloat16)
        return stack, jnp.concatenate([high, mid + pltpu.roll(low, 4, 0)], 0).astype(jnp.bfloat16)

    def word(unit, n):
        at = 2 * unit + n + LANES
        return units[at >> 7, at & (LANES - 1)]

    def block_of(unit):
        return word(unit, 0) >> BASE_BITS

    def fetch(unit):
        rights = [right_tile(word(unit, n)) for n in range(2)]
        return jnp.concatenate([r.T for r, _ in rights], 0), jnp.concatenate([r for _, r in rights], 1)

    def weigh(unit, turned):
        w = jnp.maximum(matmul(turned, lefts[block_of(unit)]), 0.0)
        high = w.astype(jnp.bfloat16)
        return jnp.concatenate([high, (w - high.astype(jnp.float32)).astype(jnp.bfloat16)], 1)

    def add(unit, right, w):
        part = matmul(right, w)
        at = pl.ds(pl.multiple_of(block_of(unit) * SUM_ROWS, SUM_ROWS), SUM_ROWS)
        sums[at, :] = sums[at, :] + (part[:, :LANES] + part[:, LANES:])

    for k in range(LEAD):
        turned_kept[k], right_kept[k] = fetch(begin * STEP + k)
    weights_kept[...] = jnp.zeros_like(weights_kept)
    partner_kept[...] = jnp.zeros_like(partner_kept)

    def group(first, many):
        fetched = [(turned_kept[k], right_kept[k]) for k in range(LEAD)]
        weighed = [(partner_kept[k], weights_kept[k]) for k in range(LAG)]
        for k in range(many):
            add(jnp.maximum(first + k - LAG, 0), *weighed[k])
            turned, right = fetched[k]
            weighed.append((right, weigh(first + k, turned)))
            fetched.append(fetch(first + k + LEAD))
        for k in range(LEAD):
            turned_kept[k], right_kept[k] = fetched[many + k]
        for k in range(LAG):
            partner_kept[k], weights_kept[k] = weighed[many + k]

    def double(number, carry):
        group((begin + 2 * number) * STEP, 2 * STEP)
        return carry

    lax.fori_loop(0, (end - begin) >> 1, double, 0)

    @pl.when(((end - begin) & 1) == 1)
    def _():
        group((end - 1) * STEP, STEP)

    for k in range(LAG):
        add(jnp.maximum(end * STEP - LAG + k, 0), partner_kept[k], weights_kept[k])


def start_list(words, units, sem):
    copy = pltpu.make_async_copy(words.at[pl.ds(0, 8)], units.at[pl.ds(0, 8)], sem)
    copy.start()

    def ready():
        copy.wait()

        @pl.when(LANES + 2 * (units[0, 1] * STEP + LEAD) > 8 * LANES)
        def _():
            more = pl.ds(8, units.shape[0] - 8)
            rest = pltpu.make_async_copy(words.at[more], units.at[more], sem)
            rest.start()
            rest.wait()

    return ready


def forces_of(blocks, points, all_sums):
    def entry(n):
        at = pl.ds(n, blocks, stride=SUM_ROWS)
        return sum(sums[at, :] for sums in all_sums)

    total = entry(4)
    forces = []
    for c in range(3):
        y = points[pl.ds(c * blocks, blocks), :]
        forces.append((2.0 * STIFFNESS) * (y * total - (entry(c) + entry(8 + c) + entry(12 + c))))
    return forces


def build_units(size, shape, codes, out):
    devices, blocks = size
    nrow, ncol, span = shape
    row, col = lax.axis_index("row"), lax.axis_index("col")
    me = row * ncol + col
    shift = blocks.bit_length() - 1
    cshift = ncol.bit_length() - 1
    wide = (nrow * blocks).bit_length() - 1
    code = codes[...]
    height = code.shape[0]
    holder = lax.broadcasted_iota(jnp.int32, code.shape, 0) // span
    by_row = holder < ncol
    valid = (code >= 0) & (holder < ncol + nrow)
    left, right = code >> wide, code & (nrow * blocks - 1)
    left_owner = jnp.where(by_row, row, holder - ncol) * ncol + (left >> shift)
    right_owner = ((right >> shift) << cshift) + jnp.where(by_row, holder, col)
    left_place, right_place = left & (blocks - 1), right & (blocks - 1)
    distinct = (left_owner != right_owner) | (left_place != right_place)
    mine = jnp.where(by_row, left_place, right_place)
    owner = jnp.where(by_row, left_owner, right_owner)
    valid = valid & (owner == me) & (by_row | distinct)
    other = jnp.where(by_row, right_owner, left_owner)
    place = jnp.where(by_row, right_place, left_place)
    slot = slot_of(other, me, devices)
    back = (devices - slot) * (4 * blocks) - place
    group = jnp.where(valid, jnp.where(slot < slot_ranges(devices)[2][0], mine, mine + blocks), -1)

    ones = jnp.bfloat16
    groups = 2 * blocks
    chosen = jnp.concatenate([(group == g).astype(jnp.float32) for g in range(groups)], 0)
    picked = chosen.astype(ones)
    one, two = lax.broadcasted_iota(jnp.int32, (LANES, LANES), 0), lax.broadcasted_iota(jnp.int32, (LANES, LANES), 1)
    before = matmul(picked, (one < two).astype(jnp.float32).astype(ones))
    totals = matmul(picked, jnp.ones((LANES, LANES), ones))
    lane = lax.broadcasted_iota(jnp.int32, code.shape, 1)
    table = jnp.zeros(code.shape, jnp.float32)
    for g in range(groups):
        table = jnp.where(lane == g, totals[g * height : (g + 1) * height], table)
    row_one, row_two = [lax.broadcasted_iota(jnp.int32, (height, height), n) for n in range(2)]
    above = matmul((row_two < row_one).astype(jnp.float32).astype(ones), table.astype(ones))
    filled = jnp.broadcast_to(above[height - 1 :] + table[height - 1 :], (8, LANES)).astype(jnp.int32)
    filled = filled + (filled & 1)
    pieces = [(filled & 63).astype(jnp.float32).astype(ones), (filled >> 6).astype(jnp.float32).astype(ones)]

    def total_over(mask):
        mask = mask.astype(jnp.float32).astype(ones)
        return matmul(pieces[0], mask) + 64.0 * matmul(pieces[1], mask)

    in_near = one < blocks
    step = 2 * STEP
    near_steps = (total_over(in_near).astype(jnp.int32) + step - 1) >> (step.bit_length() - 1)
    far_steps = (total_over(~in_near).astype(jnp.int32) + step - 1) >> (step.bit_length() - 1)
    offset = total_over((one < two) & (in_near == (two < blocks)))
    offset = offset + jnp.where(two[:8] < blocks, 0, near_steps * step).astype(jnp.float32)
    start = above + offset[:1]
    position = jnp.zeros(code.shape, jnp.float32)
    for g in range(groups):
        part = slice(g * height, (g + 1) * height)
        position = position + chosen[part] * (before[part] + start[:, g : g + 1])
    position = position.astype(jnp.int32) + LANES
    high = jnp.where(valid, position >> 7, -1)
    low = position & (LANES - 1)

    rows = out.shape[0]
    pieces = [(back & 63).astype(jnp.float32), (back >> 6).astype(jnp.float32), mine.astype(jnp.float32)]
    lane = lax.broadcasted_iota(jnp.int32, (LANES, LANES), 0)
    place = lax.broadcasted_iota(jnp.int32, (rows, LANES), 0)
    found = jnp.zeros((3 * rows, LANES), jnp.float32)
    for pair in range(0, height, 2):
        weights, spots = [], []
        for r in (pair, pair + 1):
            here = high[r : r + 1] == place
            weights.append(jnp.concatenate([jnp.where(here, p[r : r + 1], 0.0) for p in pieces], 0))
            spots.append((lane == low[r : r + 1]).astype(jnp.float32))
        weights, spots = jnp.concatenate(weights, 1).astype(ones), jnp.concatenate(spots, 1).astype(ones)
        found = found + lax.dot_general(
            weights, spots, (((1,), (1,)), ((), ())), preferred_element_type=jnp.float32
        )
    words = found.astype(jnp.int32)
    words = words[:rows] + words[rows : 2 * rows] * 64 + words[2 * rows :] * (BASE_MASK + 1)
    lane = lax.broadcasted_iota(jnp.int32, (rows, LANES), 1)
    words = jnp.where((place == 0) & (lane == 0), near_steps[:1], words)
    out[...] = jnp.where((place == 0) & (lane == 1), (near_steps + far_steps)[:1], words)


def slot_ranges(devices):
    near = near_size(devices)
    middle = near + devices // 2
    return range(2 * near), range(2 * near, 3 * near), range(3 * near, middle), range(middle, devices)


def first_kernel(size, shape, gathered, velocity, x_next, force_out, words, codes, units, sem, *scratch):
    devices, blocks = size
    nrow, ncol, span = shape
    rows = 3 * blocks + LIST_ROWS
    row, col = lax.axis_index("row"), lax.axis_index("col")
    me = row * ncol + col
    holders = [row * ncol + c for c in range(ncol)] + [r * ncol + col for r in range(nrow)]
    codes[...] = jnp.full_like(codes, -1)
    for n, holder in enumerate(holders):
        at = pl.multiple_of(slot_of(holder, me, devices) * rows + 3 * blocks, 8)
        codes[pl.ds(n * span, span), :] = gathered[pl.ds(at, LIST_ROWS), :][:span].astype(jnp.int32)

    build_units(size, shape, codes, words)
    ready = start_list(words, units, sem)
    load_points(size, [(gathered, 0, range(devices))], rows, scratch[0])
    add_pairs(size, None, units, ready, *scratch)
    forces = forces_of(blocks, scratch[0], [scratch[2]])
    for c in range(3):
        at = pl.ds(c * blocks, blocks)
        force_out[at, :] = forces[c]
        x_next[at, :] = gathered[at, :] + TIME_STEP * velocity[at, :] + (0.5 * TIME_STEP * TIME_STEP) * forces[c]


def near_kernel(size, near, part, words, sums_out, units, sem, points, lefts, *kept):
    devices, blocks = size
    ready = start_list(words, units, sem)
    ranges = slot_ranges(devices)
    load_points(size, [(near, 0, ranges[0]), (part, 0, ranges[1])], 3 * blocks, points)
    add_pairs(size, 0, units, ready, points, lefts, sums_out, *kept)


def next_kernel(size, last, near, middle, far, near_sums, velocity, force, words, x_next, v_next, *rest):
    devices, blocks = size
    if not last:
        force_out, *rest = rest
    units, sem, points, lefts, sums, *kept = rest
    ready = start_list(words, units, sem)
    ranges = slot_ranges(devices)
    pieces = [(near, 0, range(1)), (middle, len(ranges[1]), ranges[2]), (far, 0, ranges[3])]
    load_points(size, pieces, 3 * blocks, points)
    add_pairs(size, 1, units, ready, points, lefts, sums, *kept)
    forces = forces_of(blocks, points, [near_sums, sums])
    for c in range(3):
        at = pl.ds(c * blocks, blocks)
        x = near[at, :]
        v = velocity[at, :] + (0.5 * TIME_STEP) * (force[at, :] + forces[c])
        if last:
            for b in range(blocks):
                lanes = pl.ds(b * LANES, LANES)
                x_next[pl.ds(c, 1), lanes] = x[b : b + 1]
                v_next[pl.ds(c, 1), lanes] = v[b : b + 1]
        else:
            v_next[at, :] = v
            force_out[at, :] = forces[c]
            x_next[at, :] = x + TIME_STEP * v + (0.5 * TIME_STEP * TIME_STEP) * forces[c]


def body(positions, velocities, pair_lists, pair_counts):
    nrow, ncol = lax.axis_size("row"), lax.axis_size("col")
    devices = nrow * ncol
    blocks = positions.shape[1] // LANES
    pairs = pair_lists[0, 0]
    slots = pairs.shape[0]
    size = (devices, blocks)
    span = slots // LANES
    entries = LANES + (nrow + ncol) * slots + 2 * blocks + 2 * (3 * STEP + LEAD)
    unit_rows = 8 * (entries // (8 * LANES) + 1)
    code_rows = 8 * (-(-(nrow + ncol) * span // 8))
    flat = jax.ShapeDtypeStruct((3 * blocks, LANES), jnp.float32)
    whole = jax.ShapeDtypeStruct(positions.shape, jnp.float32)
    unit_list = jax.ShapeDtypeStruct((unit_rows, LANES), jnp.int32)
    vmem = pl.BlockSpec(memory_space=pltpu.VMEM)
    smem = pl.BlockSpec(memory_space=pltpu.SMEM)
    points = pltpu.VMEM(((devices + 3) * 4 * blocks, LANES), jnp.float32)
    lefts = pltpu.VMEM((blocks, 48, LANES), jnp.bfloat16)
    sums = pltpu.VMEM((blocks * SUM_ROWS, LANES), jnp.float32)
    kept = [
        pltpu.VMEM((LEAD, 2 * LANES, 48), jnp.bfloat16),
        pltpu.VMEM((LEAD, SUM_ROWS, 2 * LANES), jnp.bfloat16),
        pltpu.VMEM((LAG, 2 * LANES, 2 * LANES), jnp.bfloat16),
        pltpu.VMEM((LAG, SUM_ROWS, 2 * LANES), jnp.bfloat16),
    ]
    listed = [pltpu.SMEM((unit_rows, LANES), jnp.int32), pltpu.SemaphoreType.DMA]
    params = pltpu.CompilerParams(vmem_limit_bytes=48 * 1024 * 1024)

    def cost(share):
        flops = int(share * 4e9)
        return pl.CostEstimate(flops=flops, bytes_accessed=1 << 20, transcendentals=0)

    packed, velocity = pl.pallas_call(
        functools.partial(prepare_kernel, blocks, nrow * blocks),
        out_shape=[jax.ShapeDtypeStruct((3 * blocks + LIST_ROWS, LANES), jnp.float32), flat],
        in_specs=[vmem, vmem, vmem, smem],
        out_specs=[vmem, vmem],
        name="prepare",
    )(positions, velocities, pairs.T, pair_counts)
    near, both = gather_near(packed, devices)
    current, force, words = pl.pallas_call(
        functools.partial(first_kernel, size, (nrow, ncol, span)),
        out_shape=[flat, flat, unit_list],
        in_specs=[vmem] * 2,
        out_specs=[vmem] * 3,
        scratch_shapes=[pltpu.VMEM((code_rows, LANES), jnp.int32)] + listed + [points, lefts, sums] + kept,
        compiler_params=params,
        cost_estimate=cost(1.0),
        name="first_forces",
    )(jnp.concatenate([both, *exchange(gather_last(near, devices), devices)], 0), velocity)
    for turn in range(STEPS):
        last = turn == STEPS - 1
        near, both = gather_near(current, devices)
        parts = gather_last(near, devices)
        near_sums = pl.pallas_call(
            functools.partial(near_kernel, size),
            out_shape=jax.ShapeDtypeStruct((blocks * SUM_ROWS, LANES), jnp.float32),
            in_specs=[vmem] * 3,
            out_specs=vmem,
            scratch_shapes=listed + [points, lefts] + kept,
            compiler_params=params,
            cost_estimate=cost(0.25),
            name="near_forces",
        )(both, parts[0], words)
        parts, near_sums = lax.optimization_barrier((parts, near_sums))
        result = pl.pallas_call(
            functools.partial(next_kernel, size, last),
            out_shape=[whole] * 2 if last else [flat] * 3,
            in_specs=[vmem] * 7,
            out_specs=[vmem] * (2 if last else 3),
            scratch_shapes=listed + [points, lefts, sums] + kept,
            compiler_params=params,
            cost_estimate=cost(0.75),
            name="last_forces" if last else "next_forces",
        )(both, *exchange(parts, devices), near_sums, velocity, force, words)
        if last:
            current, velocity = result
        else:
            current, velocity, force = result
    return current, velocity


def solution(mesh):
    placed = (
        P(None, ("row", "col")),
        P(None, ("row", "col")),
        P("row", "col", None, None),
        P("row", "col"),
    )
    return jax.shard_map(
        body,
        mesh=mesh,
        in_specs=placed,
        out_specs=(P(None, ("row", "col")), P(None, ("row", "col"))),
        check_vma=False,
    )
```
